256 devices in a mesh: gx: 8 (over z), gy: 8 (over y, core), gz: 4 (over x).
Axes of the slice: x: 4, y: 4, z: 8, core: 2. Of those that a mesh axis runs over, the one named last changes fastest.
Arguments:
- adjoint_disp: float32 [3, 32, 64, 512], P(None, 'gx', 'gy', 'gz'), may hold values from -6 to 6
- matrix_tangent: float32 [6, 6], replicated, may hold values from -6 to 6
- fibre_blocks: bfloat16 [36, 512], replicated, may hold values from -24 to 24
- fibre_weights: bfloat16 [1048576, 512], P(('gx', 'gy', 'gz')), may hold values from 0.099609375 to 10
- rve_class: int32 [1048576], P(('gx', 'gy', 'gz')), may hold values from 0 to 3
- rve_helper: int32 [32, 64, 512], P('gx', 'gy', 'gz'), may hold values from 0 to 63, as said below
- rve_slot: int32 [32, 64, 512], P('gx', 'gy', 'gz'), may hold values from 0 to 4095, as said below
Outputs:
- node_force: float32 [3, 32, 64, 512], P(None, 'gx', 'gy', 'gz')
The draws below stay inside these ranges and needn't reach their ends.
Inputs may be any that keep to these rules, and one draw needn't show every extreme that they name: `rve_helper`: positions count along gx and gy with gx first. The number of points that one device sends to the owner k positions after its own (mod 64) depends only on k, is at most 128, and equals 128 for some k. `rve_slot`: for each owner and each gz plane, the points of that plane whose RVE lies with that owner name each of its 4096 rows exactly once.
All inputs are finite; a program needn't handle non-finite values.
Results may differ from the reference program's by a relative error of at most 0.0003.
Values sent between devices are 32-bit elements; how exact they have to be, the bound alone decides.
No kernel may reach another device: no remote copies, remote signals or barrier semaphores. Data moves between devices by JAX's collectives and lax.ppermute only.
A program may use at most 64 MiB of HBM per device.

```python
import math
import jax
import jax.numpy as jnp
from jax import lax

EX = 4
EY = 8
EZ = 128
FIBRES = 512
CLASSES = 4
NX = 32
NY = 64
NZ = 512
POINTS_DEV = 4096
RVE_ROWS = 1048576
N_GX = 8
N_GY = 8
N_GZ = 4
DEVICES = 256


def to_grid(values):
    values = values.reshape(N_GX, N_GY, N_GZ, EX, EY, EZ)
    return values.transpose(0, 3, 1, 4, 2, 5).reshape(EX * N_GX, EY * N_GY, EZ * N_GZ)


def assignment(key):
    owners = N_GX * N_GY
    points = EX * EY * EZ
    mean = points // owners
    key_shift, key_order, key_rank, key_label = jax.random.split(key, 4)
    spread = jax.random.randint(key_shift, (owners // 2,), -mean, mean + 1).astype(jnp.int32)
    spread = spread.at[0].set(mean)
    counts = jnp.stack([mean + spread, mean - spread], 1).reshape(owners)
    counts = jax.random.permutation(key_order, counts)
    ends = jnp.cumsum(counts).astype(jnp.int32)
    base = jnp.broadcast_to(jnp.arange(points, dtype=jnp.int32), (N_GX, N_GY, N_GZ, points))
    rank = jax.random.permutation(key_rank, base, axis=3, independent=True)
    offset = jnp.searchsorted(ends, rank, side='right').astype(jnp.int32)
    source = (jnp.arange(N_GX, dtype=jnp.int32)[:, None] * N_GY + jnp.arange(N_GY, dtype=jnp.int32)[None, :])[:, :, None, None]
    helper = ((source + offset) % owners).astype(jnp.int32)
    relabel = jax.random.permutation(key_label, base, axis=3, independent=True)
    plane = jnp.arange(N_GZ, dtype=jnp.int32)[None, None, :, None]
    slot = relabel[helper // N_GY, helper % N_GY, plane, rank].astype(jnp.int32)
    return (to_grid(helper), to_grid(slot))


def draw_rve_helper(key, part):
    return assignment(key)[0]


def draw_rve_slot(key, part):
    return assignment(key)[1]


def touch_ends(array, stream_key, least, high):
    longest = array.shape.index(max(array.shape))
    spots = []
    for shift in (0, 1):
        where = [jax.random.randint(jax.random.fold_in(stream_key, axis), (), 0, length) for axis, length in enumerate(array.shape)]
        where[longest] = (where[longest] + shift) % array.shape[longest]
        spots.append(tuple(where))
    return array.at[spots[0]].set(least).at[spots[1]].set(high)


def block_levels(stream_key, shape, pieces, smallest, largest):
    level = 1.0
    for axis_at, parts in pieces:
        draws = jax.random.uniform(jax.random.fold_in(jax.random.fold_in(stream_key, 6), axis_at), (parts,), jnp.float32, smallest / len(pieces), largest / len(pieces))
        level = level * jnp.repeat(jnp.exp(draws), shape[axis_at] // parts).reshape((-1,) + (1,) * (len(shape) - 1 - axis_at))
    return level


def normal_values(own_key, dims, scale, most, cuts=(), kind=jnp.bfloat16):
    array = jax.random.normal(own_key, dims, jnp.float32) * scale
    if len(cuts) > 0:
        array = block_levels(own_key, dims, cuts, -0.22, 0.18) * array
    return jnp.clip(array, min=-most, max=most).astype(kind)


def setup_inputs(seed: int = 0) -> dict:
    splits = jax.random.split(jax.random.key(seed), 8)
    adjoint_disp = normal_values(splits[0], (3, NX, NY, NZ), 1.0, 6.0, ((1, 8), (2, 8), (3, 4)), jnp.float32)
    matrix_tangent = normal_values(splits[1], (6, 6), 1.0, 6.0, (), jnp.float32)
    fibre_blocks = normal_values(splits[2], (36, FIBRES), 4.0, 24.0)
    fibre_weights = jnp.clip(jnp.exp(math.log(10.0) - 4.609084 * jax.random.uniform(splits[3], (RVE_ROWS, FIBRES), jnp.float32) ** block_levels(splits[3], (RVE_ROWS, FIBRES), ((0, 256),), -0.2, 0.2)), 0.099609375, 10.0).astype(jnp.bfloat16)
    rve_class = touch_ends(jax.random.randint(splits[4], (RVE_ROWS,), 0, CLASSES), jax.random.fold_in(splits[4], 1), 0, CLASSES - 1).astype(jnp.int32)
    rve_helper = draw_rve_helper(jax.random.fold_in(splits[7], 71), 0)
    rve_slot = draw_rve_slot(jax.random.fold_in(splits[7], 71), 0)
    return dict(adjoint_disp=adjoint_disp, matrix_tangent=matrix_tangent, fibre_blocks=fibre_blocks, fibre_weights=fibre_weights, rve_class=rve_class, rve_helper=rve_helper, rve_slot=rve_slot)


SIGNS = (-0.25, 0.25)


def strains_of(disp):
    size_x, size_y, size_z = disp.shape[1], disp.shape[2], disp.shape[3]
    padded = jnp.pad(disp, ((0, 0), (0, 1), (0, 1), (0, 1)))
    corner = [[[padded[:, a:a + size_x, b:b + size_y, c:c + size_z] for c in range(2)] for b in range(2)] for a in range(2)]
    grad_x = 0.25 * (sum(corner[1][b][c] for b in range(2) for c in range(2)) - sum(corner[0][b][c] for b in range(2) for c in range(2)))
    grad_y = 0.25 * (sum(corner[a][1][c] for a in range(2) for c in range(2)) - sum(corner[a][0][c] for a in range(2) for c in range(2)))
    grad_z = 0.25 * (sum(corner[a][b][1] for a in range(2) for b in range(2)) - sum(corner[a][b][0] for a in range(2) for b in range(2)))
    return jnp.stack([grad_x[0], grad_y[1], grad_z[2], grad_z[1] + grad_y[2], grad_z[0] + grad_x[2], grad_y[0] + grad_x[1]])


def forces_of(sens):
    size_x, size_y, size_z = sens.shape[1], sens.shape[2], sens.shape[3]
    along_x = jnp.stack([sens[0], sens[5], sens[4]])
    along_y = jnp.stack([sens[5], sens[1], sens[3]])
    along_z = jnp.stack([sens[4], sens[3], sens[2]])
    total = jnp.zeros((3, size_x + 1, size_y + 1, size_z + 1), jnp.float32)
    for a in range(2):
        for b in range(2):
            for c in range(2):
                piece = SIGNS[a] * along_x + SIGNS[b] * along_y + SIGNS[c] * along_z
                total = total.at[:, a:a + size_x, b:b + size_y, c:c + size_z].add(piece)
    return total[:, :size_x, :size_y, :size_z]


def tangent_block(weights, classes, blocks):
    fibres = weights.shape[1]
    active = (classes + 1) * (fibres // CLASSES)
    keep = jnp.arange(fibres, dtype=jnp.int32)[None, :] < active[:, None]
    kept = jnp.where(keep, weights.astype(jnp.float32), jnp.zeros((), jnp.float32))
    raw = lax.dot_general(blocks.astype(jnp.float32), kept, (((1,), (1,)), ((), ())),
                          precision=lax.Precision.HIGHEST, preferred_element_type=jnp.float32)
    return raw / active.astype(jnp.float32)[None, :]


def reference(adjoint_disp, matrix_tangent, fibre_blocks, fibre_weights, rve_class, rve_helper, rve_slot):
    strain = strains_of(adjoint_disp)
    weights_grouped = fibre_weights.reshape(DEVICES, POINTS_DEV, FIBRES)
    classes_grouped = rve_class.reshape(DEVICES, POINTS_DEV)
    table = lax.map(lambda pair: tangent_block(pair[0], pair[1], fibre_blocks), (weights_grouped, classes_grouped))
    plane = (jnp.arange(NZ, dtype=jnp.int32) // EZ).astype(jnp.int32)
    row = (POINTS_DEV * (N_GZ * rve_helper + plane[None, None, :]) + rve_slot).astype(jnp.int32)
    owner = (row // POINTS_DEV).astype(jnp.int32)
    local = (row % POINTS_DEV).astype(jnp.int32)
    picked = table[owner, :, local].reshape(NX, NY, NZ, 6, 6)
    matrix_part = jnp.einsum("mn,mxyz->nxyz", matrix_tangent, strain, precision=lax.Precision.HIGHEST)
    fibre_part = jnp.einsum("xyzmn,mxyz->nxyz", picked, strain, precision=lax.Precision.HIGHEST)
    sens = matrix_part + fibre_part
    return forces_of(sens)
```

```python
import functools

import jax
import jax.numpy as jnp
from jax import lax
from jax.experimental import pallas as pl
from jax.experimental.pallas import tpu as pltpu
from jax.sharding import PartitionSpec as P

CLASSES = 4
LANES = 128
STEP = 4
SMEM = pl.BlockSpec(memory_space=pltpu.SMEM)
VMEM = pl.BlockSpec(memory_space=pltpu.VMEM)
NT = (((1,), (1,)), ((), ()))


def passed_round(array, axis, by):
    devices = lax.axis_size(axis)
    return lax.ppermute(array, axis, [(i, (i + by) % devices) for i in range(devices)])


def whole_call(kernel, name, out, inputs, scratch=(), flops=0, scalars=()):
    outs = [VMEM] * len(out) if isinstance(out, (list, tuple)) else VMEM
    return pl.pallas_call(
        kernel,
        name=name,
        out_shape=out,
        in_specs=[SMEM if i in scalars else VMEM for i in range(len(inputs))],
        out_specs=outs,
        scratch_shapes=list(scratch),
        cost_estimate=pl.CostEstimate(flops=flops, bytes_accessed=1 << 20, transcendentals=0),
        compiler_params=pltpu.CompilerParams(vmem_limit_bytes=32 << 20),
    )(*inputs)


def f32(*shape):
    return jax.ShapeDtypeStruct(shape, jnp.float32)


def i32(*shape):
    return jax.ShapeDtypeStruct(shape, jnp.int32)


def iota(shape, dim):
    return lax.broadcasted_iota(jnp.int32, shape, dim)


def halves(table):
    high = table.astype(jnp.bfloat16)
    low = (table - high.astype(jnp.float32)).astype(jnp.bfloat16)
    return jnp.concatenate([high, low], 1)


def one_hot(low):
    return jnp.where(iota((LANES, LANES), 0) == low, 1.0, 0.0).astype(jnp.bfloat16)


def looked_up(table, highs, columns, start):
    products = jnp.dot(
        table, jnp.concatenate([columns, columns], 0), preferred_element_type=jnp.float32
    )
    found = []
    for i, high in enumerate(highs):
        total = jnp.full((8, LANES), start, jnp.float32)
        for row in range(table.shape[0] // 8):
            part = products[8 * row : 8 * row + 8, LANES * i : LANES * (i + 1)]
            total = jnp.where(high == row, part, total)
        found.append(total)
    return found


def spread(row):
    return jnp.broadcast_to(row, (8, LANES))


def transposed_lanes(block):
    gap = LANES - block.shape[0]
    if gap:
        block = jnp.concatenate([block, jnp.zeros((gap, LANES), block.dtype)], 0)
    return block.T


def first_layer_kernel(disp_ref, out_ref):
    out_ref[...] = transposed_lanes(disp_ref[...])[0:8]


def route_kernel(owners, helper_ref, source_ref, target_ref, member_ref, ranks_ref):
    blocks = helper_ref.shape[0]
    upper = (iota((LANES, 2 * LANES), 0) <= iota((LANES, 2 * LANES), 1)).astype(jnp.bfloat16)
    owner = iota((owners, LANES), 0)
    lane = iota((owners, LANES), 1)
    place = iota((LANES, LANES), 0)
    before = jnp.zeros((owners, LANES), jnp.float32)
    for block in range(blocks):
        helper = helper_ref[pl.ds(block, 1), :]
        member = helper == owner
        counted = jnp.dot(
            jnp.where(member, 1.0, 0.0).astype(jnp.bfloat16),
            upper,
            preferred_element_type=jnp.float32,
        )
        rank = before + counted[:, :LANES] - 1.0
        rank = jnp.sum(jnp.where(member, rank, 0.0), 0, keepdims=True).astype(jnp.int32)
        before = before + counted[:, LANES:]
        target_ref[pl.ds(block, 1), :] = helper * LANES + rank
        columns = pl.ds(block * LANES, LANES)
        member_ref[pl.ds(0, owners), columns] = jnp.where(member, float(block), 0.0).astype(
            jnp.bfloat16
        )
        member_ref[pl.ds(owners, owners), columns] = jnp.where(
            member, (lane + 1).astype(jnp.float32), 0.0
        ).astype(jnp.bfloat16)
        ranks_ref[:, columns] = jnp.where(place == rank, 1.0, 0.0).astype(jnp.bfloat16)
    found = lax.dot_general(
        member_ref[...], ranks_ref[...], NT, preferred_element_type=jnp.float32
    ).astype(jnp.int32)
    source_ref[...] = found[:owners] * LANES + found[owners:] - 1


def strain_kernel(
    owners,
    width_x,
    inside_ref,
    disp_ref,
    first_ref,
    side_ref,
    next_ref,
    source_ref,
    slot_ref,
    out_ref,
    field_ref,
):
    planes = width_x
    in_x, in_y, in_z = (inside_ref[i] != 0 for i in range(3))
    edges = transposed_lanes(
        jnp.concatenate(
            [
                first_ref[0:1],
                side_ref[24:25],
                next_ref[15:16],
                next_ref[16:17],
                jnp.zeros((4, LANES), jnp.float32),
            ],
            0,
        )
    )
    sums = {}
    for c in range(3):
        for x in range(planes + 1):
            k = c * planes + x
            if x < planes:
                here = disp_ref[pl.ds(8 * k, 8), :]
                above = next_ref[pl.ds(k, 1), :]
                spot, column = 8 * k, 0
            else:
                here = side_ref[pl.ds(8 * c, 8), :]
                above = next_ref[pl.ds(3 * planes + c, 1), :]
                spot, column = 8 * c * planes, 1
            edge = jnp.where(in_z, edges[spot : spot + 8, column : column + 1], 0.0)
            corner = jnp.where(in_z, edges[spot : spot + 1, column + 2 : column + 3], 0.0)
            if x == planes:
                here, edge = jnp.where(in_x, here, 0.0), jnp.where(in_x, edge, 0.0)
                above, corner = jnp.where(in_x, above, 0.0), jnp.where(in_x, corner, 0.0)
            above, corner = jnp.where(in_y, above, 0.0), jnp.where(in_y, corner, 0.0)
            here_z = jnp.concatenate([here[:, 1:], edge], 1)
            there = jnp.concatenate([here[1:], above], 0)
            there_z = jnp.concatenate([here_z[1:], jnp.concatenate([above[:, 1:], corner], 1)], 0)
            low, high = here + here_z, there + there_z
            sums[c, x] = (low + high, high - low, (here_z - here) + (there_z - there))
    for x in range(planes):
        grad_x = [0.25 * (sums[c, x + 1][0] - sums[c, x][0]) for c in range(3)]
        grad_y = [0.25 * (sums[c, x + 1][1] + sums[c, x][1]) for c in range(3)]
        grad_z = [0.25 * (sums[c, x + 1][2] + sums[c, x][2]) for c in range(3)]
        slot = slot_ref[pl.ds(8 * x, 8), :].astype(jnp.float32)
        fields = (
            grad_x[0],
            grad_y[1],
            grad_z[2],
            grad_z[1] + grad_y[2],
            grad_z[0] + grad_x[2],
            grad_y[0] + grad_x[1],
            slot,
            slot,
        )
        for f, field in enumerate(fields):
            field_ref[pl.ds(64 * x + f, 8, stride=8), :] = field
    table = halves(field_ref[...])
    for owner in range(0, owners, STEP):
        rows = [source_ref[pl.ds(o, 1), :] for o in range(owner, owner + STEP)]
        columns = jnp.concatenate([one_hot(row & (LANES - 1)) for row in rows], 1)
        found = looked_up(table, [spread(row >> 7) for row in rows], columns, -1.0)
        for i in range(STEP):
            out_ref[owner + i] = found[i]


def tangent_kernel(weights_ref, class_ref, blocks_ref, matrix_ref, out_ref):
    points = weights_ref.shape[0]
    fibres = blocks_ref[...].astype(jnp.float32)
    gap = jnp.zeros((2, fibres.shape[1]), jnp.float32)
    pieces = []
    for m in range(6):
        pieces += [fibres[6 * m : 6 * m + 6], gap]
    fibres = jnp.concatenate(pieces, 0).astype(jnp.bfloat16)
    row = iota((8, LANES), 0)
    matrix = []
    for m in range(6):
        column = jnp.zeros((8, LANES), jnp.float32)
        for n in range(6):
            column = jnp.where(row == n, matrix_ref[m, n], column)
        matrix.append(column)
    matrix = jnp.concatenate(matrix, 0)
    chunk = 1024
    for start in range(0, points, chunk):
        parts = []
        for group in range(CLASSES):
            columns = slice(LANES * group, LANES * (group + 1))
            parts.append(
                lax.dot_general(
                    fibres[:, columns],
                    weights_ref[pl.ds(start, chunk), columns],
                    NT,
                    preferred_element_type=jnp.float32,
                )
            )
        for block in range(chunk // LANES):
            lanes = slice(LANES * block, LANES * (block + 1))
            level = class_ref[pl.ds(start // LANES + block, 1), :]
            total = parts[0][:, lanes]
            for group in range(1, CLASSES):
                total = total + jnp.where(level >= group, parts[group][:, lanes], 0.0)
            scale = 1.0 / ((level + 1) * LANES).astype(jnp.float32)
            out_ref[:, pl.ds(start + LANES * block, LANES)] = total * scale + matrix


def respond_kernel(arrived_ref, tangent_ref, out_ref, member_ref, lows_ref, answer_ref):
    owners = arrived_ref.shape[0]
    blocks = tangent_ref.shape[1] // LANES
    rows = iota((blocks, LANES), 0)
    lane = (iota((blocks, LANES), 1) + 1).astype(jnp.float32)
    slots = []
    for sender in range(owners):
        slot = arrived_ref[sender, 6:7, :].astype(jnp.int32)
        slots.append(slot)
        named = rows == (slot >> 7)
        columns = pl.ds(sender * LANES, LANES)
        member_ref[pl.ds(0, blocks), columns] = jnp.where(named, float(sender), 0.0).astype(
            jnp.bfloat16
        )
        member_ref[pl.ds(blocks, blocks), columns] = jnp.where(named, lane, 0.0).astype(jnp.bfloat16)
        lows_ref[:, columns] = one_hot(slot & (LANES - 1))
    where = lax.dot_general(
        member_ref[...], lows_ref[...], NT, preferred_element_type=jnp.float32
    ).astype(jnp.int32)

    table = halves(arrived_ref[...].reshape(8 * owners, LANES))
    for block in range(0, blocks, STEP):
        steps = range(block, block + STEP)
        columns = jnp.concatenate([one_hot(where[blocks + b : blocks + b + 1] - 1) for b in steps], 1)
        found = looked_up(table, [spread(where[b : b + 1]) for b in steps], columns, 0.0)
        for i, b in enumerate(steps):
            total = jnp.zeros((8, LANES), jnp.float32)
            for m in range(6):
                tangent = tangent_ref[pl.ds(8 * m, 8), pl.ds(b * LANES, LANES)]
                total = total + tangent * spread(found[i][m : m + 1])
            answer_ref[pl.ds(8 * b, 8), :] = total

    table = halves(answer_ref[...])
    for sender in range(0, owners, STEP):
        columns = lows_ref[:, pl.ds(sender * LANES, STEP * LANES)]
        highs = [spread(slot >> 7) for slot in slots[sender : sender + STEP]]
        found = looked_up(table, highs, columns, 0.0)
        for i in range(STEP):
            out_ref[sender + i] = found[i]


def collect_kernel(returned_ref, target_ref, sens_ref, last_ref, point_ref):
    owners = returned_ref.shape[0]
    blocks = target_ref.shape[0]
    table = halves(returned_ref[...].reshape(8 * owners, LANES))
    for block in range(0, blocks, STEP):
        rows = [target_ref[pl.ds(b, 1), :] for b in range(block, block + STEP)]
        columns = jnp.concatenate([one_hot(row & (LANES - 1)) for row in rows], 1)
        found = looked_up(table, [spread(row >> 7) for row in rows], columns, 0.0)
        for i in range(STEP):
            point_ref[pl.ds(8 * (block + i), 8), :] = found[i]
    for f in range(6):
        sens_ref[pl.ds(blocks * f, blocks), :] = point_ref[pl.ds(f, blocks, stride=8), :]
    half = 3 * blocks
    for part in range(2):
        turned = transposed_lanes(sens_ref[pl.ds(half * part, half), :])
        last_ref[pl.ds(part, 1), :] = turned[LANES - 1 : LANES]
    last_ref[pl.ds(2, 6), :] = jnp.zeros((6, LANES), jnp.float32)


def force_kernel(width_x, inside_ref, sens_ref, last_ref, side_ref, prior_ref, out_ref):
    planes = width_x
    blocks = 8 * planes
    fields = 6
    in_x, in_y, in_z = (inside_ref[i] != 0 for i in range(3, 6))
    rows = jnp.concatenate(
        [
            last_ref[0:2],
            side_ref[48:50],
            prior_ref[30:34],
        ],
        0,
    )
    edges = transposed_lanes(rows)
    sums = {}
    for f in range(fields):
        for x in range(-1, planes):
            part, g = f // 3, f % 3
            if x >= 0:
                here = sens_ref[pl.ds(blocks * f + 8 * x, 8), :]
                above = prior_ref[pl.ds(planes * f + x, 1), :]
                spot, column = blocks * g + 8 * x, part
            else:
                here = side_ref[pl.ds(8 * f, 8), :]
                above = prior_ref[pl.ds(planes * fields + f, 1), :]
                spot, column = blocks * g + 8 * (planes - 1), part + 2
            edge = jnp.where(in_z, edges[spot : spot + 8, column : column + 1], 0.0)
            corner = jnp.where(in_z, edges[spot + 7 : spot + 8, column + 4 : column + 5], 0.0)
            if x < 0:
                here, edge = jnp.where(in_x, here, 0.0), jnp.where(in_x, edge, 0.0)
                above, corner = jnp.where(in_x, above, 0.0), jnp.where(in_x, corner, 0.0)
            above, corner = jnp.where(in_y, above, 0.0), jnp.where(in_y, corner, 0.0)
            here_z = jnp.concatenate([edge, here[:, :-1]], 1)
            there = jnp.concatenate([above, here[:-1]], 0)
            there_z = jnp.concatenate([jnp.concatenate([corner, above[:, :-1]], 1), here_z[:-1]], 0)
            low, high = there + there_z, here + here_z
            sums[f, x] = (low + high, low - high, (here_z - here) + (there_z - there))

    def both(f, x, kind):
        return sums[f, x][kind] + sums[f, x - 1][kind]

    def jump(f, x):
        return sums[f, x - 1][0] - sums[f, x][0]

    along = ((0, 5, 4), (5, 1, 3), (4, 3, 2))
    for d in range(3):
        for x in range(planes):
            force = jump(along[d][0], x) + both(along[d][1], x, 1) + both(along[d][2], x, 2)
            out_ref[pl.ds(blocks * d + 8 * x, 8), :] = 0.25 * force


def per_device(
    adjoint_disp, matrix_tangent, fibre_blocks, fibre_weights, rve_class, rve_helper, rve_slot
):
    owners = lax.axis_size("gx") * lax.axis_size("gy")
    width_x, width_y, width_z = adjoint_disp.shape[1:]
    points = width_x * width_y * width_z
    blocks = points // LANES
    fibres = fibre_weights.shape[1]
    disp = adjoint_disp.reshape(3 * blocks, LANES)
    helper = rve_helper.reshape(blocks, LANES)
    slot = rve_slot.reshape(blocks, LANES)

    places = [lax.axis_index(axis) for axis in ("gx", "gy", "gz")]
    ends = [lax.axis_size(axis) - 1 for axis in ("gx", "gy", "gz")]
    inside = jnp.stack(
        [place < end for place, end in zip(places, ends)] + [place > 0 for place in places]
    ).astype(jnp.int32)

    with jax.named_scope("lift"):
        first = whole_call(first_layer_kernel, "first_layer", f32(8, LANES), (disp,))
        first = passed_round(first, "gz", -1)
        side = jnp.concatenate([adjoint_disp[:, 0].reshape(24, LANES), first], 0)
        side = passed_round(side, "gx", -1)
        next_y = jnp.concatenate(
            [
                adjoint_disp[:, :, 0].reshape(3 * width_x, LANES),
                side[0:24:8],
                first[0:1],
                side[24:25],
            ],
            0,
        )
        next_y = passed_round(next_y, "gy", -1)

    with jax.named_scope("route"):
        source, target = whole_call(
            functools.partial(route_kernel, owners),
            "route",
            [i32(owners, LANES), i32(blocks, LANES)],
            (helper,),
            [
                pltpu.VMEM((2 * owners, points), jnp.bfloat16),
                pltpu.VMEM((LANES, points), jnp.bfloat16),
            ],
            flops=2 * points * LANES * 2 * owners,
        )

    with jax.named_scope("strain"):
        buckets = whole_call(
            functools.partial(strain_kernel, owners, width_x),
            "strain",
            f32(owners, 8, LANES),
            (inside, disp, first, side, next_y, source, slot),
            [pltpu.VMEM((8 * blocks, LANES), jnp.float32)],
            scalars=(0,),
        )

    with jax.named_scope("tangent"):
        tangent = whole_call(
            tangent_kernel,
            "tangent",
            f32(48, points),
            (fibre_weights, rve_class.reshape(blocks, LANES), fibre_blocks, matrix_tangent),
            flops=2 * 256 * points * fibres,
            scalars=(3,),
        )

    with jax.named_scope("exchange"):
        arrived = lax.all_to_all(buckets, ("gx", "gy"), split_axis=0, concat_axis=0, tiled=True)

    with jax.named_scope("respond"):
        answer = whole_call(
            respond_kernel,
            "respond",
            f32(owners, 8, LANES),
            (arrived, tangent),
            [
                pltpu.VMEM((2 * blocks, owners * LANES), jnp.bfloat16),
                pltpu.VMEM((LANES, owners * LANES), jnp.bfloat16),
                pltpu.VMEM((8 * blocks, LANES), jnp.float32),
            ],
        )

    with jax.named_scope("return"):
        returned = lax.all_to_all(answer, ("gx", "gy"), split_axis=0, concat_axis=0, tiled=True)

    with jax.named_scope("collect"):
        sens, last = whole_call(
            collect_kernel,
            "collect",
            [f32(6 * blocks, LANES), f32(8, LANES)],
            (returned, target),
            [pltpu.VMEM((8 * blocks, LANES), jnp.float32)],
        )

    with jax.named_scope("settle"):
        sens_grid = sens.reshape(6, width_x, width_y, LANES)
        last = passed_round(last, "gz", 1)
        side = jnp.concatenate([sens_grid[:, -1].reshape(48, LANES), last], 0)
        side = passed_round(side, "gx", 1)
        prior = jnp.concatenate(
            [
                sens_grid[:, :, -1].reshape(6 * width_x, LANES),
                side[7:48:8],
                last[0:2],
                side[48:50],
            ],
            0,
        )
        prior = passed_round(prior, "gy", 1)
        force = whole_call(
            functools.partial(force_kernel, width_x),
            "force",
            f32(3 * blocks, LANES),
            (inside, sens, last, side, prior),
            scalars=(0,),
        )
    return force.reshape(3, width_x, width_y, width_z)


def solution(mesh):
    in_specs = (
        P(None, "gx", "gy", "gz"),
        P(),
        P(),
        P(("gx", "gy", "gz"), None),
        P(("gx", "gy", "gz")),
        P("gx", "gy", "gz"),
        P("gx", "gy", "gz"),
    )
    out_specs = P(None, "gx", "gy", "gz")
    return jax.shard_map(
        per_device, mesh=mesh, in_specs=in_specs, out_specs=out_specs, check_vma=False
    )
```

```python
import functools

import jax
import jax.numpy as jnp
from jax import lax
from jax.experimental import pallas as pl
from jax.experimental.pallas import tpu as pltpu
from jax.sharding import PartitionSpec as P

CLASSES = 4
LANES = 128
STEP = 4
SMEM = pl.BlockSpec(memory_space=pltpu.SMEM)
HBM = pl.BlockSpec(memory_space=pltpu.HBM)
VMEM = pl.BlockSpec(memory_space=pltpu.VMEM)
NT = (((1,), (1,)), ((), ()))


def passed_round(array, axis, by):
    devices = lax.axis_size(axis)
    return lax.ppermute(array, axis, [(i, (i + by) % devices) for i in range(devices)])


def exchanged(array, owners, axes):
    flat = array.reshape(owners, 1, -1)
    flat = lax.all_to_all(flat, axes, split_axis=0, concat_axis=0, tiled=True)
    return flat.reshape(array.shape)


def whole_call(kernel, name, out, inputs, scratch=(), flops=0, places=None):
    return pl.pallas_call(
        kernel,
        name=name,
        out_shape=out,
        in_specs=places or [VMEM] * len(inputs),
        out_specs=[VMEM] * len(out) if isinstance(out, (list, tuple)) else VMEM,
        scratch_shapes=list(scratch),
        cost_estimate=pl.CostEstimate(flops=flops, bytes_accessed=1 << 20, transcendentals=0),
        compiler_params=pltpu.CompilerParams(vmem_limit_bytes=16 << 20),
    )(*inputs)


def f32(*shape):
    return jax.ShapeDtypeStruct(shape, jnp.float32)


def i32(*shape):
    return jax.ShapeDtypeStruct(shape, jnp.int32)


def iota(shape, dim):
    return lax.broadcasted_iota(jnp.int32, shape, dim)


def halves(table):
    high = table.astype(jnp.bfloat16)
    low = (table - high.astype(jnp.float32)).astype(jnp.bfloat16)
    return jnp.concatenate([high, low], 1)


def one_hot(low):
    place = iota((LANES, LANES), 0).astype(jnp.float32).astype(jnp.bfloat16)
    low = jnp.broadcast_to(low.astype(jnp.float32).astype(jnp.bfloat16), (LANES, LANES))
    return jnp.where(place == low, jnp.ones((), jnp.bfloat16), jnp.zeros((), jnp.bfloat16))


def looked_up(table, fields, highs, columns):
    products = jnp.dot(
        table, jnp.concatenate([columns, columns], 0), preferred_element_type=jnp.float32
    )
    rows = table.shape[0] // fields
    place = iota((8, LANES), 0)
    found = []
    for i, high in enumerate(highs):
        lanes = slice(LANES * i, LANES * (i + 1))
        named = [place == high - 8 * g for g in range(rows // 8)]
        values = []
        for f in range(fields):
            total = jnp.zeros((8, LANES), jnp.float32)
            for g, here in enumerate(named):
                start = rows * f + 8 * g
                total = jnp.where(here, products[start : start + 8, lanes], total)
            for shift in (4, 2, 1):
                total = total + pltpu.roll(total, shift, 0)
            values.append(total)
        found.append(values)
    return found


def stacked(values):
    place = iota((8, LANES), 0)
    tile = values[0]
    for f in range(1, len(values)):
        tile = jnp.where(place == f, values[f], tile)
    return tile


def spread(row):
    return jnp.broadcast_to(row, (8, LANES))


def transposed_lanes(block):
    gap = LANES - block.shape[0]
    if gap:
        block = jnp.concatenate([block, jnp.zeros((gap, LANES), block.dtype)], 0)
    return block.T


def fetch_kernel(count, *refs):
    inputs, (first_ref, *kept, sems) = refs[:count], refs[count:]
    copies = [
        pltpu.make_async_copy(source, target, sems.at[i])
        for i, (source, target) in enumerate(zip(inputs, kept))
    ]
    for copy in copies:
        copy.start()
    copies[0].wait()
    first_ref[...] = transposed_lanes(kept[0][...])[0:8]
    for copy in copies[1:]:
        copy.wait()


def route_kernel(
    owners, helper_ref, weights_hbm, high_ref, low_ref, rank_ref, weights_ref, member_ref, ranks_ref, sem
):
    copy = pltpu.make_async_copy(weights_hbm, weights_ref, sem)
    copy.start()
    blocks = helper_ref.shape[0]
    upper = (iota((LANES, 2 * LANES), 0) <= iota((LANES, 2 * LANES), 1)).astype(jnp.bfloat16)
    owner = iota((owners, LANES), 0)
    lane = iota((owners, LANES), 1)
    before = jnp.zeros((owners, LANES), jnp.float32)
    for block in range(blocks):
        member = helper_ref[pl.ds(block, 1), :] == owner
        counted = jnp.dot(
            jnp.where(member, 1.0, 0.0).astype(jnp.bfloat16),
            upper,
            preferred_element_type=jnp.float32,
        )
        rank = before + counted[:, :LANES] - 1.0
        rank = jnp.sum(jnp.where(member, rank, 0.0), 0, keepdims=True)
        before = before + counted[:, LANES:]
        columns = pl.ds(block * LANES, LANES)
        member_ref[pl.ds(0, owners), columns] = jnp.where(member, float(block), 0.0).astype(
            jnp.bfloat16
        )
        member_ref[pl.ds(owners, owners), columns] = jnp.where(
            member, (lane + 1).astype(jnp.float32), 0.0
        ).astype(jnp.bfloat16)
        rank_ref[pl.ds(block, 1), :] = rank
        ranks_ref[:, columns] = one_hot(rank)
    found = lax.dot_general(
        member_ref[...], ranks_ref[...], NT, preferred_element_type=jnp.float32
    ).astype(jnp.int32)
    lows = found[owners:] - 1
    high_ref[...] = jnp.where(lows < 0, -1, found[:owners])
    for bucket in range(owners):
        low_ref[:, pl.ds(bucket * LANES, LANES)] = one_hot(lows[bucket : bucket + 1])
    copy.wait()


def strain_kernel(
    owners,
    width_x,
    inside_ref,
    disp_ref,
    first_ref,
    side_ref,
    next_ref,
    high_ref,
    low_ref,
    slot_ref,
    out_ref,
    field_ref,
):
    planes = width_x
    in_x, in_y, in_z = (inside_ref[i] != 0 for i in range(3))
    edges = transposed_lanes(
        jnp.concatenate(
            [
                first_ref[0:1],
                side_ref[24:25],
                next_ref[15:16],
                next_ref[16:17],
                jnp.zeros((4, LANES), jnp.float32),
            ],
            0,
        )
    )
    sums = {}
    for c in range(3):
        for x in range(planes + 1):
            k = c * planes + x
            if x < planes:
                here = disp_ref[pl.ds(8 * k, 8), :]
                above = next_ref[pl.ds(k, 1), :]
                spot, column = 8 * k, 0
            else:
                here = side_ref[pl.ds(8 * c, 8), :]
                above = next_ref[pl.ds(3 * planes + c, 1), :]
                spot, column = 8 * c * planes, 1
            edge = jnp.where(in_z, edges[spot : spot + 8, column : column + 1], 0.0)
            corner = jnp.where(in_z, edges[spot : spot + 1, column + 2 : column + 3], 0.0)
            if x == planes:
                here, edge = jnp.where(in_x, here, 0.0), jnp.where(in_x, edge, 0.0)
                above, corner = jnp.where(in_x, above, 0.0), jnp.where(in_x, corner, 0.0)
            above, corner = jnp.where(in_y, above, 0.0), jnp.where(in_y, corner, 0.0)
            here_z = jnp.concatenate([here[:, 1:], edge], 1)
            there = jnp.concatenate([here[1:], above], 0)
            there_z = jnp.concatenate([here_z[1:], jnp.concatenate([above[:, 1:], corner], 1)], 0)
            low, high = here + here_z, there + there_z
            sums[c, x] = (low + high, high - low, (here_z - here) + (there_z - there))
    for x in range(planes):
        grad_x = [0.25 * (sums[c, x + 1][0] - sums[c, x][0]) for c in range(3)]
        grad_y = [0.25 * (sums[c, x + 1][1] + sums[c, x][1]) for c in range(3)]
        grad_z = [0.25 * (sums[c, x + 1][2] + sums[c, x][2]) for c in range(3)]
        slot = (slot_ref[pl.ds(8 * x, 8), :] + 1).astype(jnp.float32)
        fields = (
            grad_x[0],
            grad_y[1],
            grad_z[2],
            grad_z[1] + grad_y[2],
            grad_z[0] + grad_x[2],
            grad_y[0] + grad_x[1],
            slot,
        )
        for f, field in enumerate(fields):
            field_ref[pl.ds(8 * (planes * f + x), 8), :] = field
    table = halves(field_ref[...])
    for owner in range(0, owners, STEP):
        steps = range(owner, owner + STEP)
        highs = [spread(high_ref[pl.ds(o, 1), :]) for o in steps]
        columns = low_ref[:, pl.ds(owner * LANES, STEP * LANES)]
        for o, found in zip(steps, looked_up(table, 7, highs, columns)):
            out_ref[pl.ds(7 * o, 7), :] = stacked(found)[0:7]


def tangent_kernel(weights_ref, class_ref, blocks_ref, matrix_ref, out_ref, square_ref):
    fibres = blocks_ref[...].astype(jnp.float32)
    gap = jnp.zeros((2, fibres.shape[1]), jnp.float32)
    pieces = []
    for m in range(6):
        pieces += [fibres[6 * m : 6 * m + 6], gap]
    fibres = jnp.concatenate(pieces, 0).astype(jnp.bfloat16)
    square_ref[...] = jnp.zeros(square_ref.shape, jnp.float32)
    square_ref[0:6, 0:6] = matrix_ref[...]
    turned = transposed_lanes(square_ref[...])
    matrix = jnp.concatenate(
        [jnp.broadcast_to(turned[0:8, m : m + 1], (8, LANES)) for m in range(6)], 0
    )
    chunk = 1024
    for start in range(0, out_ref.shape[1], chunk):
        parts = []
        for group in range(CLASSES):
            columns = slice(LANES * group, LANES * (group + 1))
            parts.append(
                lax.dot_general(
                    fibres[:, columns],
                    weights_ref[pl.ds(start, chunk), columns],
                    NT,
                    preferred_element_type=jnp.float32,
                )
            )
        for block in range(chunk // LANES):
            lanes = slice(LANES * block, LANES * (block + 1))
            level = class_ref[pl.ds(start // LANES + block, 1), :]
            total = parts[0][:, lanes]
            for group in range(1, CLASSES):
                total = total + jnp.where(level >= group, parts[group][:, lanes], 0.0)
            scale = 1.0 / ((level + 1) * LANES).astype(jnp.float32)
            out_ref[:, pl.ds(start + LANES * block, LANES)] = total * scale + matrix


def fields_first(packed_ref, width):
    rows = packed_ref.shape[0] // width
    return halves(
        jnp.concatenate([packed_ref[pl.ds(f, rows, stride=width), :] for f in range(6)], 0)
    )


def respond_kernel(
    arrived_ref, tangent_ref, out_ref, member_ref, lows_ref, answer_ref
):
    owners = arrived_ref.shape[0] // 7
    blocks = tangent_ref.shape[1] // LANES
    rows = iota((blocks, LANES), 0)
    lane = (iota((blocks, LANES), 1) + 1).astype(jnp.float32)
    slots = []
    for sender in range(owners):
        slot = arrived_ref[pl.ds(7 * sender + 6, 1), :].astype(jnp.int32) - 1
        slots.append(slot)
        named = rows == (slot >> 7)
        columns = pl.ds(sender * LANES, LANES)
        member_ref[pl.ds(0, blocks), columns] = jnp.where(named, float(sender), 0.0).astype(
            jnp.bfloat16
        )
        member_ref[pl.ds(blocks, blocks), columns] = jnp.where(named, lane, 0.0).astype(jnp.bfloat16)
        lows_ref[:, columns] = one_hot(slot & (LANES - 1))
    where = lax.dot_general(
        member_ref[...], lows_ref[...], NT, preferred_element_type=jnp.float32
    ).astype(jnp.int32)

    table = fields_first(arrived_ref, 7)
    for block in range(0, blocks, STEP):
        steps = range(block, block + STEP)
        columns = jnp.concatenate([one_hot(where[blocks + b : blocks + b + 1] - 1) for b in steps], 1)
        found = looked_up(table, 6, [spread(where[b : b + 1]) for b in steps], columns)
        for i, b in enumerate(steps):
            lanes = pl.ds(b * LANES, LANES)
            total = jnp.zeros((8, LANES), jnp.float32)
            for m in range(6):
                total = total + tangent_ref[pl.ds(8 * m, 8), lanes] * found[i][m]
            answer_ref[pl.ds(8 * b, 8), :] = total

    table = fields_first(answer_ref, 8)
    for sender in range(0, owners, STEP):
        columns = lows_ref[:, pl.ds(sender * LANES, STEP * LANES)]
        highs = [spread(slot >> 7) for slot in slots[sender : sender + STEP]]
        for i, found in enumerate(looked_up(table, 6, highs, columns)):
            out_ref[pl.ds(6 * (sender + i), 6), :] = stacked(found)[0:6]


def collect_kernel(returned_ref, helper_ref, rank_ref, sens_ref, last_ref):
    blocks = helper_ref.shape[0]
    table = fields_first(returned_ref, 6)
    for block in range(0, blocks, STEP):
        steps = range(block, block + STEP)
        highs = [spread(helper_ref[pl.ds(b, 1), :]) for b in steps]
        columns = jnp.concatenate([one_hot(rank_ref[pl.ds(b, 1), :]) for b in steps], 1)
        for i, found in enumerate(looked_up(table, 6, highs, columns)):
            for f in range(6):
                sens_ref[pl.ds(blocks * f + block + i, 1), :] = found[f][0:1]
    half = 3 * blocks
    for part in range(2):
        turned = transposed_lanes(sens_ref[pl.ds(half * part, half), :])
        last_ref[pl.ds(part, 1), :] = turned[LANES - 1 : LANES]
    last_ref[pl.ds(2, 6), :] = jnp.zeros((6, LANES), jnp.float32)


def force_kernel(width_x, inside_ref, sens_ref, last_ref, side_ref, prior_ref, out_ref):
    planes = width_x
    blocks = 8 * planes
    fields = 6
    in_x, in_y, in_z = (inside_ref[i] != 0 for i in range(3, 6))
    rows = jnp.concatenate(
        [
            last_ref[0:2],
            side_ref[48:50],
            prior_ref[30:34],
        ],
        0,
    )
    edges = transposed_lanes(rows)
    sums = {}
    for f in range(fields):
        for x in range(-1, planes):
            part, g = f // 3, f % 3
            if x >= 0:
                here = sens_ref[pl.ds(blocks * f + 8 * x, 8), :]
                above = prior_ref[pl.ds(planes * f + x, 1), :]
                spot, column = blocks * g + 8 * x, part
            else:
                here = side_ref[pl.ds(8 * f, 8), :]
                above = prior_ref[pl.ds(planes * fields + f, 1), :]
                spot, column = blocks * g + 8 * (planes - 1), part + 2
            edge = jnp.where(in_z, edges[spot : spot + 8, column : column + 1], 0.0)
            corner = jnp.where(in_z, edges[spot + 7 : spot + 8, column + 4 : column + 5], 0.0)
            if x < 0:
                here, edge = jnp.where(in_x, here, 0.0), jnp.where(in_x, edge, 0.0)
                above, corner = jnp.where(in_x, above, 0.0), jnp.where(in_x, corner, 0.0)
            above, corner = jnp.where(in_y, above, 0.0), jnp.where(in_y, corner, 0.0)
            here_z = jnp.concatenate([edge, here[:, :-1]], 1)
            there = jnp.concatenate([above, here[:-1]], 0)
            there_z = jnp.concatenate([jnp.concatenate([corner, above[:, :-1]], 1), here_z[:-1]], 0)
            low, high = there + there_z, here + here_z
            sums[f, x] = (low + high, low - high, (here_z - here) + (there_z - there))

    def both(f, x, kind):
        return sums[f, x][kind] + sums[f, x - 1][kind]

    def jump(f, x):
        return sums[f, x - 1][0] - sums[f, x][0]

    along = ((0, 5, 4), (5, 1, 3), (4, 3, 2))
    for d in range(3):
        for x in range(planes):
            force = jump(along[d][0], x) + both(along[d][1], x, 1) + both(along[d][2], x, 2)
            out_ref[pl.ds(blocks * d + 8 * x, 8), :] = 0.25 * force


def per_device(
    adjoint_disp, matrix_tangent, fibre_blocks, fibre_weights, rve_class, rve_helper, rve_slot
):
    owners = lax.axis_size("gx") * lax.axis_size("gy")
    width_x, width_y, width_z = adjoint_disp.shape[1:]
    points = width_x * width_y * width_z
    blocks = points // LANES
    fibres = fibre_weights.shape[1]
    places = [lax.axis_index(axis) for axis in ("gx", "gy", "gz")]
    ends = [lax.axis_size(axis) - 1 for axis in ("gx", "gy", "gz")]
    inside = jnp.stack(
        [place < end for place, end in zip(places, ends)] + [place > 0 for place in places]
    ).astype(jnp.int32)

    with jax.named_scope("fetch"):
        inputs = (
            adjoint_disp.reshape(3 * blocks, LANES),
            rve_helper.reshape(blocks, LANES),
            rve_slot.reshape(blocks, LANES),
            rve_class.reshape(blocks, LANES),
            fibre_blocks,
            matrix_tangent,
        )
        kept = [jax.ShapeDtypeStruct(a.shape, a.dtype) for a in inputs]
        first, disp, helper, slot, level, fibre, matrix = whole_call(
            functools.partial(fetch_kernel, len(inputs)),
            "fetch",
            [f32(8, LANES)] + kept,
            [pltpu.with_memory_space_constraint(a, pltpu.HBM) for a in inputs],
            [pltpu.SemaphoreType.DMA((len(inputs),))],
            places=[HBM] * len(inputs),
        )
        disp_grid = disp.reshape(3, width_x, width_y, LANES)

    with jax.named_scope("route"):
        high, low, rank, weights = whole_call(
            functools.partial(route_kernel, owners),
            "route",
            [
                i32(owners, LANES),
                jax.ShapeDtypeStruct((LANES, owners * LANES), jnp.bfloat16),
                f32(blocks, LANES),
                jax.ShapeDtypeStruct(fibre_weights.shape, fibre_weights.dtype),
            ],
            (helper, pltpu.with_memory_space_constraint(fibre_weights, pltpu.HBM)),
            [
                pltpu.VMEM((2 * owners, points), jnp.bfloat16),
                pltpu.VMEM((LANES, points), jnp.bfloat16),
                pltpu.SemaphoreType.DMA(()),
            ],
            flops=2 * points * LANES * 2 * owners,
            places=[VMEM, HBM],
        )

    with jax.named_scope("tangent"):
        tangent = whole_call(
            tangent_kernel,
            "tangent",
            f32(48, points),
            (weights, level, fibre, matrix),
            [pltpu.VMEM((8, LANES), jnp.float32)],
            flops=2 * 256 * points * fibres,
        )

    with jax.named_scope("lift"):
        first = passed_round(first, "gz", -1)
        first, high, low, rank = lax.optimization_barrier((first, high, low, rank))
        side = jnp.concatenate([disp_grid[:, 0].reshape(24, LANES), first], 0)
        side = passed_round(side, "gx", -1)
        side, tangent = lax.optimization_barrier((side, tangent))
        next_y = jnp.concatenate(
            [
                disp_grid[:, :, 0].reshape(3 * width_x, LANES),
                side[0:24:8],
                first[0:1],
                side[24:25],
            ],
            0,
        )
        next_y = passed_round(next_y, "gy", -1)

    with jax.named_scope("strain"):
        buckets = whole_call(
            functools.partial(strain_kernel, owners, width_x),
            "strain",
            f32(owners * 7, LANES),
            (inside, disp, first, side, next_y, high, low, slot),
            [pltpu.VMEM((7 * blocks, LANES), jnp.float32)],
            places=[SMEM] + [VMEM] * 7,
        )

    with jax.named_scope("exchange"):
        arrived = exchanged(buckets, owners, ("gx", "gy"))

    with jax.named_scope("respond"):
        answer = whole_call(
            respond_kernel,
            "respond",
            f32(owners * 6, LANES),
            (arrived, tangent),
            [
                pltpu.VMEM((2 * blocks, owners * LANES), jnp.bfloat16),
                pltpu.VMEM((LANES, owners * LANES), jnp.bfloat16),
                pltpu.VMEM((8 * blocks, LANES), jnp.float32),
            ],
        )

    with jax.named_scope("return"):
        returned = exchanged(answer, owners, ("gx", "gy"))

    with jax.named_scope("collect"):
        sens, last = whole_call(
            collect_kernel,
            "collect",
            [f32(6 * blocks, LANES), f32(8, LANES)],
            (returned, helper, rank),
        )

    with jax.named_scope("settle"):
        sens_grid = sens.reshape(6, width_x, width_y, LANES)
        last = passed_round(last, "gz", 1)
        side = jnp.concatenate([sens_grid[:, -1].reshape(48, LANES), last], 0)
        side = passed_round(side, "gx", 1)
        prior = jnp.concatenate(
            [
                sens_grid[:, :, -1].reshape(6 * width_x, LANES),
                side[7:48:8],
                last[0:2],
                side[48:50],
            ],
            0,
        )
        prior = passed_round(prior, "gy", 1)
        force = whole_call(
            functools.partial(force_kernel, width_x),
            "force",
            f32(3 * blocks, LANES),
            (inside, sens, last, side, prior),
            places=[SMEM] + [VMEM] * 4,
        )
    return force.reshape(3, width_x, width_y, width_z)


def solution(mesh):
    in_specs = (
        P(None, "gx", "gy", "gz"),
        P(),
        P(),
        P(("gx", "gy", "gz"), None),
        P(("gx", "gy", "gz")),
        P("gx", "gy", "gz"),
        P("gx", "gy", "gz"),
    )
    out_specs = P(None, "gx", "gy", "gz")
    return jax.shard_map(
        per_device, mesh=mesh, in_specs=in_specs, out_specs=out_specs, check_vma=False
    )
```

```python
import functools

import jax
import jax.numpy as jnp
from jax import lax
from jax.experimental import pallas as pl
from jax.experimental.pallas import tpu as pltpu
from jax.sharding import PartitionSpec as P

CLASSES = 4
LANES = 128
STEP = 4
SMEM = pl.BlockSpec(memory_space=pltpu.SMEM)
HBM = pl.BlockSpec(memory_space=pltpu.HBM)
VMEM = pl.BlockSpec(memory_space=pltpu.VMEM)
NT = (((1,), (1,)), ((), ()))


def passed_round(array, axes, by):
    pairs = [(0, 0)]
    for axis in axes:
        size = lax.axis_size(axis)
        pairs = [
            (source * size + i, target * size + (i + by) % size)
            for source, target in pairs
            for i in range(size)
        ]
    return lax.ppermute(array, axes, pairs)


def passed_on(array, axes, by):
    pairs = [(0, 0)]
    for axis in axes:
        size = lax.axis_size(axis)
        pairs = [
            (source * size + i, target * size + i + by)
            for source, target in pairs
            for i in range(size)
            if 0 <= i + by < size
        ]
    return lax.ppermute(array, axes, pairs)


def exchanged(array, owners, axes):
    flat = array.reshape(owners, 1, -1)
    flat = lax.all_to_all(flat, axes, split_axis=0, concat_axis=0, tiled=True)
    return flat.reshape(array.shape)


def whole_call(kernel, name, out, inputs, scratch=(), flops=0, places=None):
    return pl.pallas_call(
        kernel,
        name=name,
        out_shape=out,
        in_specs=places or [VMEM] * len(inputs),
        out_specs=[VMEM] * len(out) if isinstance(out, (list, tuple)) else VMEM,
        scratch_shapes=list(scratch),
        cost_estimate=pl.CostEstimate(flops=flops, bytes_accessed=1 << 20, transcendentals=0),
        compiler_params=pltpu.CompilerParams(vmem_limit_bytes=16 << 20),
    )(*inputs)


def f32(*shape):
    return jax.ShapeDtypeStruct(shape, jnp.float32)


def i32(*shape):
    return jax.ShapeDtypeStruct(shape, jnp.int32)


def iota(shape, dim):
    return lax.broadcasted_iota(jnp.int32, shape, dim)


def halves(table):
    high = table.astype(jnp.bfloat16)
    low = (table - high.astype(jnp.float32)).astype(jnp.bfloat16)
    return jnp.concatenate([high, low], 1)


def one_hot(low):
    place = iota((LANES, LANES), 0).astype(jnp.float32).astype(jnp.bfloat16)
    low = jnp.broadcast_to(low.astype(jnp.float32).astype(jnp.bfloat16), (LANES, LANES))
    return jnp.where(place == low, jnp.ones((), jnp.bfloat16), jnp.zeros((), jnp.bfloat16))


def looked_up(table, fields, highs, columns):
    products = jnp.dot(
        table, jnp.concatenate([columns, columns], 0), preferred_element_type=jnp.float32
    )
    rows = table.shape[0] // fields
    place = iota((8, LANES), 0)
    found = []
    for i, high in enumerate(highs):
        lanes = slice(LANES * i, LANES * (i + 1))
        named = [place == high - 8 * g for g in range(rows // 8)]
        values = []
        for f in range(fields):
            total = jnp.zeros((8, LANES), jnp.float32)
            for g, here in enumerate(named):
                start = rows * f + 8 * g
                total = jnp.where(here, products[start : start + 8, lanes], total)
            for shift in (4, 2, 1):
                total = total + pltpu.roll(total, shift, 0)
            values.append(total)
        found.append(values)
    return found


def stacked(values):
    place = iota((8, LANES), 0)
    tile = values[0]
    for f in range(1, len(values)):
        tile = jnp.where(place == f, values[f], tile)
    return tile


def spread(row):
    return jnp.broadcast_to(row, (8, LANES))


def transposed_lanes(block):
    gap = LANES - block.shape[0]
    if gap:
        block = jnp.concatenate([block, jnp.zeros((gap, LANES), block.dtype)], 0)
    return block.T


def fetch_kernel(count, *refs):
    inputs, (first_ref, *kept, sems) = refs[:count], refs[count:]
    copies = [
        pltpu.make_async_copy(source, target, sems.at[i])
        for i, (source, target) in enumerate(zip(inputs, kept))
    ]
    for copy in copies:
        copy.start()
    copies[0].wait()
    first_ref[...] = transposed_lanes(kept[0][...])[0:8]
    for copy in copies[1:]:
        copy.wait()


def route_kernel(
    owners, helper_ref, weights_hbm, high_ref, low_ref, rank_ref, weights_ref, member_ref, ranks_ref, sem
):
    copy = pltpu.make_async_copy(weights_hbm.at[pl.ds(0, weights_ref.shape[0])], weights_ref, sem)
    copy.start()
    blocks = helper_ref.shape[0]
    upper = (iota((LANES, 2 * LANES), 0) <= iota((LANES, 2 * LANES), 1)).astype(jnp.bfloat16)
    owner = iota((owners, LANES), 0)
    lane = iota((owners, LANES), 1)
    before = jnp.zeros((owners, LANES), jnp.float32)
    for block in range(blocks):
        member = helper_ref[pl.ds(block, 1), :] == owner
        counted = jnp.dot(
            jnp.where(member, 1.0, 0.0).astype(jnp.bfloat16),
            upper,
            preferred_element_type=jnp.float32,
        )
        rank = before + counted[:, :LANES] - 1.0
        rank = jnp.sum(jnp.where(member, rank, 0.0), 0, keepdims=True)
        before = before + counted[:, LANES:]
        columns = pl.ds(block * LANES, LANES)
        member_ref[pl.ds(0, owners), columns] = jnp.where(member, float(block), 0.0).astype(
            jnp.bfloat16
        )
        member_ref[pl.ds(owners, owners), columns] = jnp.where(
            member, (lane + 1).astype(jnp.float32), 0.0
        ).astype(jnp.bfloat16)
        rank_ref[pl.ds(block, 1), :] = rank
        ranks_ref[:, columns] = one_hot(rank)
    found = lax.dot_general(
        member_ref[...], ranks_ref[...], NT, preferred_element_type=jnp.float32
    ).astype(jnp.int32)
    lows = found[owners:] - 1
    high_ref[...] = jnp.where(lows < 0, -1, found[:owners])
    for bucket in range(owners):
        low_ref[:, pl.ds(bucket * LANES, LANES)] = one_hot(lows[bucket : bucket + 1])
    copy.wait()


def strain_kernel(
    owners,
    width_x,
    inside_ref,
    disp_ref,
    first_ref,
    side_ref,
    corner_ref,
    next_ref,
    high_ref,
    low_ref,
    slot_ref,
    out_ref,
    field_ref,
):
    planes = width_x
    in_x, in_y, in_z = (inside_ref[i] != 0 for i in range(3))
    edges = transposed_lanes(
        jnp.concatenate(
            [
                first_ref[0:1],
                corner_ref[0:1],
                next_ref[15:16],
                next_ref[16:17],
                jnp.zeros((4, LANES), jnp.float32),
            ],
            0,
        )
    )
    sums = {}
    for c in range(3):
        for x in range(planes + 1):
            k = c * planes + x
            if x < planes:
                here = disp_ref[pl.ds(8 * k, 8), :]
                above = next_ref[pl.ds(k, 1), :]
                spot, column = 8 * k, 0
            else:
                here = side_ref[pl.ds(8 * c, 8), :]
                above = next_ref[pl.ds(3 * planes + c, 1), :]
                spot, column = 8 * c * planes, 1
            edge = jnp.where(in_z, edges[spot : spot + 8, column : column + 1], 0.0)
            corner = jnp.where(in_z, edges[spot : spot + 1, column + 2 : column + 3], 0.0)
            if x == planes:
                here, edge = jnp.where(in_x, here, 0.0), jnp.where(in_x, edge, 0.0)
                above, corner = jnp.where(in_x, above, 0.0), jnp.where(in_x, corner, 0.0)
            above, corner = jnp.where(in_y, above, 0.0), jnp.where(in_y, corner, 0.0)
            here_z = jnp.concatenate([here[:, 1:], edge], 1)
            there = jnp.concatenate([here[1:], above], 0)
            there_z = jnp.concatenate([here_z[1:], jnp.concatenate([above[:, 1:], corner], 1)], 0)
            low, high = here + here_z, there + there_z
            sums[c, x] = (low + high, high - low, (here_z - here) + (there_z - there))
    for x in range(planes):
        grad_x = [0.25 * (sums[c, x + 1][0] - sums[c, x][0]) for c in range(3)]
        grad_y = [0.25 * (sums[c, x + 1][1] + sums[c, x][1]) for c in range(3)]
        grad_z = [0.25 * (sums[c, x + 1][2] + sums[c, x][2]) for c in range(3)]
        slot = (slot_ref[pl.ds(8 * x, 8), :] + 1).astype(jnp.float32)
        fields = (
            grad_x[0],
            grad_y[1],
            grad_z[2],
            grad_z[1] + grad_y[2],
            grad_z[0] + grad_x[2],
            grad_y[0] + grad_x[1],
            slot,
        )
        for f, field in enumerate(fields):
            field_ref[pl.ds(8 * (planes * f + x), 8), :] = field
    table = halves(field_ref[...])
    for owner in range(0, owners, STEP):
        steps = range(owner, owner + STEP)
        highs = [spread(high_ref[pl.ds(o, 1), :]) for o in steps]
        columns = low_ref[:, pl.ds(owner * LANES, STEP * LANES)]
        for o, found in zip(steps, looked_up(table, 7, highs, columns)):
            out_ref[pl.ds(7 * o, 7), :] = stacked(found)[0:7]


def tangent_kernel(first, weights_ref, class_ref, blocks_ref, matrix_ref, out_ref, square_ref):
    tangents(first, weights_ref, [], class_ref, blocks_ref, matrix_ref, out_ref, square_ref)


def fetched_tangent_kernel(
    first, weights_hbm, class_ref, blocks_ref, matrix_ref, out_ref, square_ref, weights_ref, sems
):
    chunk = weights_ref.shape[0] // sems.shape[0]
    copies = [
        pltpu.make_async_copy(
            weights_hbm.at[pl.ds(first + chunk * i, chunk)],
            weights_ref.at[pl.ds(chunk * i, chunk)],
            sems.at[i],
        )
        for i in range(sems.shape[0])
    ]
    for copy in copies:
        copy.start()
    tangents(first, weights_ref, copies, class_ref, blocks_ref, matrix_ref, out_ref, square_ref)


def tangents(first, weights_ref, copies, class_ref, blocks_ref, matrix_ref, out_ref, square_ref):
    fibres = blocks_ref[...].astype(jnp.float32)
    gap = jnp.zeros((2, fibres.shape[1]), jnp.float32)
    pieces = []
    for m in range(6):
        pieces += [fibres[6 * m : 6 * m + 6], gap]
    fibres = jnp.concatenate(pieces, 0).astype(jnp.bfloat16)
    square_ref[...] = jnp.zeros(square_ref.shape, jnp.float32)
    square_ref[0:6, 0:6] = matrix_ref[...]
    turned = transposed_lanes(square_ref[...])
    matrix = jnp.concatenate(
        [jnp.broadcast_to(turned[0:8, m : m + 1], (8, LANES)) for m in range(6)], 0
    )
    chunk = 1024
    for i, start in enumerate(range(0, weights_ref.shape[0], chunk)):
        if copies:
            copies[i].wait()
        parts = []
        for group in range(CLASSES):
            columns = slice(LANES * group, LANES * (group + 1))
            parts.append(
                lax.dot_general(
                    fibres[:, columns],
                    weights_ref[pl.ds(start, chunk), columns],
                    NT,
                    preferred_element_type=jnp.float32,
                )
            )
        for block in range(chunk // LANES):
            lanes = slice(LANES * block, LANES * (block + 1))
            level = class_ref[pl.ds((first + start) // LANES + block, 1), :]
            total = parts[0][:, lanes]
            for group in range(1, CLASSES):
                total = total + jnp.where(level >= group, parts[group][:, lanes], 0.0)
            scale = 1.0 / ((level + 1) * LANES).astype(jnp.float32)
            out_ref[:, pl.ds(start + LANES * block, LANES)] = total * scale + matrix


def fields_first(packed_ref, width):
    rows = packed_ref.shape[0] // width
    return halves(
        jnp.concatenate([packed_ref[pl.ds(f, rows, stride=width), :] for f in range(6)], 0)
    )


def respond_kernel(
    arrived_ref, early_ref, late_ref, out_ref, member_ref, lows_ref, answer_ref
):
    owners = arrived_ref.shape[0] // 7
    half = early_ref.shape[1] // LANES
    blocks = 2 * half
    rows = iota((blocks, LANES), 0)
    lane = (iota((blocks, LANES), 1) + 1).astype(jnp.float32)
    slots = []
    for sender in range(owners):
        slot = arrived_ref[pl.ds(7 * sender + 6, 1), :].astype(jnp.int32) - 1
        slots.append(slot)
        named = rows == (slot >> 7)
        columns = pl.ds(sender * LANES, LANES)
        member_ref[pl.ds(0, blocks), columns] = jnp.where(named, float(sender), 0.0).astype(
            jnp.bfloat16
        )
        member_ref[pl.ds(blocks, blocks), columns] = jnp.where(named, lane, 0.0).astype(jnp.bfloat16)
        lows_ref[:, columns] = one_hot(slot & (LANES - 1))
    where = lax.dot_general(
        member_ref[...], lows_ref[...], NT, preferred_element_type=jnp.float32
    ).astype(jnp.int32)

    table = fields_first(arrived_ref, 7)
    for block in range(0, blocks, STEP):
        steps = range(block, block + STEP)
        columns = jnp.concatenate([one_hot(where[blocks + b : blocks + b + 1] - 1) for b in steps], 1)
        found = looked_up(table, 6, [spread(where[b : b + 1]) for b in steps], columns)
        for i, b in enumerate(steps):
            tangent_ref = early_ref if b < half else late_ref
            lanes = pl.ds(b % half * LANES, LANES)
            total = jnp.zeros((8, LANES), jnp.float32)
            for m in range(6):
                total = total + tangent_ref[pl.ds(8 * m, 8), lanes] * found[i][m]
            answer_ref[pl.ds(8 * b, 8), :] = total

    table = fields_first(answer_ref, 8)
    for sender in range(0, owners, STEP):
        columns = lows_ref[:, pl.ds(sender * LANES, STEP * LANES)]
        highs = [spread(slot >> 7) for slot in slots[sender : sender + STEP]]
        for i, found in enumerate(looked_up(table, 6, highs, columns)):
            out_ref[pl.ds(6 * (sender + i), 6), :] = stacked(found)[0:6]


def collect_kernel(returned_ref, helper_ref, rank_ref, sens_ref, last_ref):
    blocks = helper_ref.shape[0]
    table = fields_first(returned_ref, 6)
    for block in range(0, blocks, STEP):
        steps = range(block, block + STEP)
        highs = [spread(helper_ref[pl.ds(b, 1), :]) for b in steps]
        columns = jnp.concatenate([one_hot(rank_ref[pl.ds(b, 1), :]) for b in steps], 1)
        for i, found in enumerate(looked_up(table, 6, highs, columns)):
            for f in range(6):
                sens_ref[pl.ds(blocks * f + block + i, 1), :] = found[f][0:1]
    half = 3 * blocks
    for part in range(2):
        turned = transposed_lanes(sens_ref[pl.ds(half * part, half), :])
        last_ref[pl.ds(part, 1), :] = turned[LANES - 1 : LANES]
    last_ref[pl.ds(2, 6), :] = jnp.zeros((6, LANES), jnp.float32)


def force_kernel(width_x, inside_ref, sens_ref, last_ref, side_ref, corner_ref, prior_ref, out_ref):
    planes = width_x
    blocks = 8 * planes
    fields = 6
    in_x, in_y, in_z = (inside_ref[i] != 0 for i in range(3, 6))
    rows = jnp.concatenate(
        [
            last_ref[0:2],
            corner_ref[0:2],
            prior_ref[30:34],
        ],
        0,
    )
    edges = transposed_lanes(rows)
    sums = {}
    for f in range(fields):
        for x in range(-1, planes):
            part, g = f // 3, f % 3
            if x >= 0:
                here = sens_ref[pl.ds(blocks * f + 8 * x, 8), :]
                above = prior_ref[pl.ds(planes * f + x, 1), :]
                spot, column = blocks * g + 8 * x, part
            else:
                here = side_ref[pl.ds(8 * f, 8), :]
                above = prior_ref[pl.ds(planes * fields + f, 1), :]
                spot, column = blocks * g + 8 * (planes - 1), part + 2
            edge = jnp.where(in_z, edges[spot : spot + 8, column : column + 1], 0.0)
            corner = jnp.where(in_z, edges[spot + 7 : spot + 8, column + 4 : column + 5], 0.0)
            if x < 0:
                here, edge = jnp.where(in_x, here, 0.0), jnp.where(in_x, edge, 0.0)
                above, corner = jnp.where(in_x, above, 0.0), jnp.where(in_x, corner, 0.0)
            above, corner = jnp.where(in_y, above, 0.0), jnp.where(in_y, corner, 0.0)
            here_z = jnp.concatenate([edge, here[:, :-1]], 1)
            there = jnp.concatenate([above, here[:-1]], 0)
            there_z = jnp.concatenate([jnp.concatenate([corner, above[:, :-1]], 1), here_z[:-1]], 0)
            low, high = there + there_z, here + here_z
            sums[f, x] = (low + high, low - high, (here_z - here) + (there_z - there))

    def both(f, x, kind):
        return sums[f, x][kind] + sums[f, x - 1][kind]

    def jump(f, x):
        return sums[f, x - 1][0] - sums[f, x][0]

    along = ((0, 5, 4), (5, 1, 3), (4, 3, 2))
    for d in range(3):
        for x in range(planes):
            force = jump(along[d][0], x) + both(along[d][1], x, 1) + both(along[d][2], x, 2)
            out_ref[pl.ds(blocks * d + 8 * x, 8), :] = 0.25 * force


def per_device(
    adjoint_disp, matrix_tangent, fibre_blocks, fibre_weights, rve_class, rve_helper, rve_slot
):
    owners = lax.axis_size("gx") * lax.axis_size("gy")
    width_x, width_y, width_z = adjoint_disp.shape[1:]
    points = width_x * width_y * width_z
    blocks = points // LANES
    fibres = fibre_weights.shape[1]
    places = [lax.axis_index(axis) for axis in ("gx", "gy", "gz")]
    ends = [lax.axis_size(axis) - 1 for axis in ("gx", "gy", "gz")]
    inside = jnp.stack(
        [place < end for place, end in zip(places, ends)] + [place > 0 for place in places]
    ).astype(jnp.int32)

    with jax.named_scope("fetch"):
        inputs = (
            adjoint_disp.reshape(3 * blocks, LANES),
            rve_helper.reshape(blocks, LANES),
            rve_slot.reshape(blocks, LANES),
            rve_class.reshape(blocks, LANES),
            fibre_blocks,
            matrix_tangent,
        )
        kept = [jax.ShapeDtypeStruct(a.shape, a.dtype) for a in inputs]
        first, disp, helper, slot, level, fibre, matrix = whole_call(
            functools.partial(fetch_kernel, len(inputs)),
            "fetch",
            [f32(8, LANES)] + kept,
            [pltpu.with_memory_space_constraint(a, pltpu.HBM) for a in inputs],
            [pltpu.SemaphoreType.DMA((len(inputs),))],
            places=[HBM] * len(inputs),
        )
        disp_grid = disp.reshape(3, width_x, width_y, LANES)

    with jax.named_scope("route"):
        weights_hbm = pltpu.with_memory_space_constraint(fibre_weights, pltpu.HBM)
        high, low, rank, weights = whole_call(
            functools.partial(route_kernel, owners),
            "route",
            [
                i32(owners, LANES),
                jax.ShapeDtypeStruct((LANES, owners * LANES), jnp.bfloat16),
                f32(blocks, LANES),
                jax.ShapeDtypeStruct((points // 2, fibres), fibre_weights.dtype),
            ],
            (helper, weights_hbm),
            [
                pltpu.VMEM((2 * owners, points), jnp.bfloat16),
                pltpu.VMEM((LANES, points), jnp.bfloat16),
                pltpu.SemaphoreType.DMA(()),
            ],
            flops=2 * points * LANES * 2 * owners,
            places=[VMEM, HBM],
        )

    with jax.named_scope("tangent"):
        half = points // 2
        early = whole_call(
            functools.partial(tangent_kernel, 0),
            "early_tangent",
            f32(48, half),
            (weights, level, fibre, matrix),
            [pltpu.VMEM((8, LANES), jnp.float32)],
            flops=256 * points * fibres,
        )
        late = whole_call(
            functools.partial(fetched_tangent_kernel, half),
            "late_tangent",
            f32(48, half),
            (weights_hbm, level, fibre, matrix),
            [
                pltpu.VMEM((8, LANES), jnp.float32),
                pltpu.VMEM((half, fibres), jnp.bfloat16),
                pltpu.SemaphoreType.DMA((2,)),
            ],
            flops=256 * points * fibres,
            places=[HBM, VMEM, VMEM, VMEM],
        )

    with jax.named_scope("lift"):
        side = passed_round(disp_grid[:, 0].reshape(24, LANES), ("gx",), -1)
        corner = passed_round(first, ("gx", "gz"), -1)
        first = passed_round(first, ("gz",), -1)
        side, corner, first, high, low, rank, early, inside = lax.optimization_barrier(
            (side, corner, first, high, low, rank, early, inside)
        )
        next_y = jnp.concatenate(
            [
                disp_grid[:, :, 0].reshape(3 * width_x, LANES),
                side[0:24:8],
                first[0:1],
                corner[0:1],
            ],
            0,
        )
        next_y = passed_round(next_y, ("gy",), -1)
        next_y, late = lax.optimization_barrier((next_y, late))

    with jax.named_scope("strain"):
        buckets = whole_call(
            functools.partial(strain_kernel, owners, width_x),
            "strain",
            f32(owners * 7, LANES),
            (inside, disp, first, side, corner, next_y, high, low, slot),
            [pltpu.VMEM((7 * blocks, LANES), jnp.float32)],
            places=[SMEM] + [VMEM] * 8,
        )

    with jax.named_scope("exchange"):
        arrived = exchanged(buckets, owners, ("gx", "gy"))

    with jax.named_scope("respond"):
        answer = whole_call(
            respond_kernel,
            "respond",
            f32(owners * 6, LANES),
            (arrived, early, late),
            [
                pltpu.VMEM((2 * blocks, owners * LANES), jnp.bfloat16),
                pltpu.VMEM((LANES, owners * LANES), jnp.bfloat16),
                pltpu.VMEM((8 * blocks, LANES), jnp.float32),
            ],
        )

    with jax.named_scope("return"):
        returned = exchanged(answer, owners, ("gx", "gy"))

    with jax.named_scope("collect"):
        sens, last = whole_call(
            collect_kernel,
            "collect",
            [f32(6 * blocks, LANES), f32(8, LANES)],
            (returned, helper, rank),
        )

    with jax.named_scope("settle"):
        sens_grid = sens.reshape(6, width_x, width_y, LANES)
        side = passed_round(sens_grid[:, -1].reshape(48, LANES), ("gx",), 1)
        corner = passed_on(last, ("gx", "gz"), 1)
        last = passed_round(last, ("gz",), 1)
        prior = jnp.concatenate(
            [
                sens_grid[:, :, -1].reshape(6 * width_x, LANES),
                side[7:48:8],
                last[0:2],
                corner[0:2],
            ],
            0,
        )
        prior = passed_on(prior, ("gy",), 1)
        force = whole_call(
            functools.partial(force_kernel, width_x),
            "force",
            f32(3 * blocks, LANES),
            (inside, sens, last, side, corner, prior),
            places=[SMEM] + [VMEM] * 5,
        )
    return force.reshape(3, width_x, width_y, width_z)


def solution(mesh):
    in_specs = (
        P(None, "gx", "gy", "gz"),
        P(),
        P(),
        P(("gx", "gy", "gz"), None),
        P(("gx", "gy", "gz")),
        P("gx", "gy", "gz"),
        P("gx", "gy", "gz"),
    )
    out_specs = P(None, "gx", "gy", "gz")
    return jax.shard_map(
        per_device, mesh=mesh, in_specs=in_specs, out_specs=out_specs, check_vma=False
    )
```

```python
import functools

import jax
import jax.numpy as jnp
from jax import lax
from jax.experimental import pallas as pl
from jax.experimental.pallas import tpu as pltpu
from jax.sharding import PartitionSpec as P

CLASSES = 4
LANES = 128
STEP = 4
SMEM = pl.BlockSpec(memory_space=pltpu.SMEM)
HBM = pl.BlockSpec(memory_space=pltpu.HBM)
VMEM = pl.BlockSpec(memory_space=pltpu.VMEM)
NT = (((1,), (1,)), ((), ()))


def passed_round(array, axes, by):
    pairs = [(0, 0)]
    for axis in axes:
        size = lax.axis_size(axis)
        pairs = [
            (source * size + i, target * size + (i + by) % size)
            for source, target in pairs
            for i in range(size)
        ]
    return lax.ppermute(array, axes, pairs)


def passed_on(array, axes, by):
    pairs = [(0, 0)]
    for axis in axes:
        size = lax.axis_size(axis)
        pairs = [
            (source * size + i, target * size + i + by)
            for source, target in pairs
            for i in range(size)
            if 0 <= i + by < size
        ]
    return lax.ppermute(array, axes, pairs)


def exchanged(array, owners, axes):
    flat = array.reshape(owners, 1, -1)
    flat = lax.all_to_all(flat, axes, split_axis=0, concat_axis=0, tiled=True)
    return flat.reshape(array.shape)


def whole_call(kernel, name, out, inputs, scratch=(), flops=0, places=None):
    return pl.pallas_call(
        kernel,
        name=name,
        out_shape=out,
        in_specs=places or [VMEM] * len(inputs),
        out_specs=[VMEM] * len(out) if isinstance(out, (list, tuple)) else VMEM,
        scratch_shapes=list(scratch),
        cost_estimate=pl.CostEstimate(flops=flops, bytes_accessed=1 << 20, transcendentals=0),
        compiler_params=pltpu.CompilerParams(vmem_limit_bytes=16 << 20),
    )(*inputs)


def f32(*shape):
    return jax.ShapeDtypeStruct(shape, jnp.float32)


def i32(*shape):
    return jax.ShapeDtypeStruct(shape, jnp.int32)


def iota(shape, dim):
    return lax.broadcasted_iota(jnp.int32, shape, dim)


def halves(table):
    high = table.astype(jnp.bfloat16)
    low = (table - high.astype(jnp.float32)).astype(jnp.bfloat16)
    return jnp.concatenate([high, low], 1)


def one_hot(low):
    place = iota((LANES, LANES), 0).astype(jnp.float32).astype(jnp.bfloat16)
    low = jnp.broadcast_to(low.astype(jnp.float32).astype(jnp.bfloat16), (LANES, LANES))
    return jnp.where(place == low, jnp.ones((), jnp.bfloat16), jnp.zeros((), jnp.bfloat16))


def looked_up(table, fields, highs, columns):
    products = jnp.dot(
        table, jnp.concatenate([columns, columns], 0), preferred_element_type=jnp.float32
    )
    rows = table.shape[0] // fields
    place = iota((8, LANES), 0)
    found = []
    for i, high in enumerate(highs):
        lanes = slice(LANES * i, LANES * (i + 1))
        named = [place == high - 8 * g for g in range(rows // 8)]
        values = []
        for f in range(fields):
            total = jnp.zeros((8, LANES), jnp.float32)
            for g, here in enumerate(named):
                start = rows * f + 8 * g
                total = jnp.where(here, products[start : start + 8, lanes], total)
            for shift in (4, 2, 1):
                total = total + pltpu.roll(total, shift, 0)
            values.append(total)
        found.append(values)
    return found


def stacked(values):
    place = iota((8, LANES), 0)
    tile = values[0]
    for f in range(1, len(values)):
        tile = jnp.where(place == f, values[f], tile)
    return tile


def spread(row):
    return jnp.broadcast_to(row, (8, LANES))


def transposed_lanes(block):
    gap = LANES - block.shape[0]
    if gap:
        block = jnp.concatenate([block, jnp.zeros((gap, LANES), block.dtype)], 0)
    return block.T


def fetch_kernel(count, *refs):
    inputs, (first_ref, *kept, sems) = refs[:count], refs[count:]
    copies = [
        pltpu.make_async_copy(source, target, sems.at[i])
        for i, (source, target) in enumerate(zip(inputs, kept))
    ]
    for copy in copies:
        copy.start()
    copies[0].wait()
    first_ref[...] = transposed_lanes(kept[0][...])[0:8]
    for copy in copies[1:]:
        copy.wait()


def last_lanes(block):
    tile = transposed_lanes(block)[LANES - 8 :]
    rows = block.shape[0]
    return (tile + pltpu.roll(tile, rows, 1) + pltpu.roll(tile, 2 * rows, 1))[7:8]


def route_kernel(
    owners,
    helper_ref,
    weights_hbm,
    high_ref,
    low_ref,
    rank_ref,
    edge_ref,
    weights_ref,
    member_ref,
    ranks_ref,
    sem,
):
    copy = pltpu.make_async_copy(weights_hbm.at[pl.ds(0, weights_ref.shape[0])], weights_ref, sem)
    copy.start()
    blocks = helper_ref.shape[0]
    upper = (iota((LANES, 2 * LANES), 0) <= iota((LANES, 2 * LANES), 1)).astype(jnp.bfloat16)
    owner = iota((owners, LANES), 0)
    lane = iota((owners, LANES), 1)
    before = jnp.zeros((owners, LANES), jnp.float32)
    for block in range(blocks):
        member = helper_ref[pl.ds(block, 1), :] == owner
        counted = jnp.dot(
            jnp.where(member, 1.0, 0.0).astype(jnp.bfloat16),
            upper,
            preferred_element_type=jnp.float32,
        )
        rank = before + counted[:, :LANES] - 1.0
        rank = jnp.sum(jnp.where(member, rank, 0.0), 0, keepdims=True)
        before = before + counted[:, LANES:]
        columns = pl.ds(block * LANES, LANES)
        member_ref[pl.ds(0, owners), columns] = jnp.where(member, float(block), 0.0).astype(
            jnp.bfloat16
        )
        member_ref[pl.ds(owners, owners), columns] = jnp.where(
            member, (lane + 1).astype(jnp.float32), 0.0
        ).astype(jnp.bfloat16)
        rank_ref[pl.ds(block, 1), :] = rank
        ranks_ref[:, columns] = one_hot(rank)
    found = lax.dot_general(
        member_ref[...], ranks_ref[...], NT, preferred_element_type=jnp.float32
    ).astype(jnp.int32)
    lows = found[owners:] - 1
    high_ref[...] = jnp.where(lows < 0, -1, found[:owners])
    for bucket in range(owners):
        low_ref[:, pl.ds(bucket * LANES, LANES)] = one_hot(lows[bucket : bucket + 1])
    edge_ref[...] = jnp.concatenate(
        [
            last_lanes(helper_ref[...].astype(jnp.float32)),
            last_lanes(rank_ref[...]),
            jnp.zeros((6, LANES), jnp.float32),
        ],
        0,
    )
    copy.wait()


def strain_kernel(
    owners,
    width_x,
    inside_ref,
    disp_ref,
    first_ref,
    side_ref,
    corner_ref,
    next_ref,
    high_ref,
    low_ref,
    slot_ref,
    out_ref,
    field_ref,
):
    planes = width_x
    in_x, in_y, in_z = (inside_ref[i] != 0 for i in range(3))
    edges = transposed_lanes(
        jnp.concatenate(
            [
                first_ref[0:1],
                corner_ref[0:1],
                next_ref[15:16],
                next_ref[16:17],
                jnp.zeros((4, LANES), jnp.float32),
            ],
            0,
        )
    )
    sums = {}
    for c in range(3):
        for x in range(planes + 1):
            k = c * planes + x
            if x < planes:
                here = disp_ref[pl.ds(8 * k, 8), :]
                above = next_ref[pl.ds(k, 1), :]
                spot, column = 8 * k, 0
            else:
                here = side_ref[pl.ds(8 * c, 8), :]
                above = next_ref[pl.ds(3 * planes + c, 1), :]
                spot, column = 8 * c * planes, 1
            edge = jnp.where(in_z, edges[spot : spot + 8, column : column + 1], 0.0)
            corner = jnp.where(in_z, edges[spot : spot + 1, column + 2 : column + 3], 0.0)
            if x == planes:
                here, edge = jnp.where(in_x, here, 0.0), jnp.where(in_x, edge, 0.0)
                above, corner = jnp.where(in_x, above, 0.0), jnp.where(in_x, corner, 0.0)
            above, corner = jnp.where(in_y, above, 0.0), jnp.where(in_y, corner, 0.0)
            here_z = jnp.concatenate([here[:, 1:], edge], 1)
            there = jnp.concatenate([here[1:], above], 0)
            there_z = jnp.concatenate([here_z[1:], jnp.concatenate([above[:, 1:], corner], 1)], 0)
            low, high = here + here_z, there + there_z
            sums[c, x] = (low + high, high - low, (here_z - here) + (there_z - there))
    for x in range(planes):
        grad_x = [0.25 * (sums[c, x + 1][0] - sums[c, x][0]) for c in range(3)]
        grad_y = [0.25 * (sums[c, x + 1][1] + sums[c, x][1]) for c in range(3)]
        grad_z = [0.25 * (sums[c, x + 1][2] + sums[c, x][2]) for c in range(3)]
        slot = (slot_ref[pl.ds(8 * x, 8), :] + 1).astype(jnp.float32)
        fields = (
            grad_x[0],
            grad_y[1],
            grad_z[2],
            grad_z[1] + grad_y[2],
            grad_z[0] + grad_x[2],
            grad_y[0] + grad_x[1],
            slot,
        )
        for f, field in enumerate(fields):
            field_ref[pl.ds(8 * (planes * f + x), 8), :] = field
    table = halves(field_ref[...])
    for owner in range(0, owners, STEP):
        steps = range(owner, owner + STEP)
        highs = [spread(high_ref[pl.ds(o, 1), :]) for o in steps]
        columns = low_ref[:, pl.ds(owner * LANES, STEP * LANES)]
        for o, found in zip(steps, looked_up(table, 7, highs, columns)):
            out_ref[pl.ds(7 * o, 7), :] = stacked(found)[0:7]


def tangent_kernel(first, weights_ref, class_ref, blocks_ref, matrix_ref, out_ref, square_ref):
    tangents(first, weights_ref, [], class_ref, blocks_ref, matrix_ref, out_ref, square_ref)


def fetched_tangent_kernel(
    first, weights_hbm, class_ref, blocks_ref, matrix_ref, out_ref, square_ref, weights_ref, sems
):
    chunk = weights_ref.shape[0] // sems.shape[0]
    copies = [
        pltpu.make_async_copy(
            weights_hbm.at[pl.ds(first + chunk * i, chunk)],
            weights_ref.at[pl.ds(chunk * i, chunk)],
            sems.at[i],
        )
        for i in range(sems.shape[0])
    ]
    for copy in copies:
        copy.start()
    tangents(first, weights_ref, copies, class_ref, blocks_ref, matrix_ref, out_ref, square_ref)


def tangents(first, weights_ref, copies, class_ref, blocks_ref, matrix_ref, out_ref, square_ref):
    fibres = blocks_ref[...].astype(jnp.float32)
    gap = jnp.zeros((2, fibres.shape[1]), jnp.float32)
    pieces = []
    for m in range(6):
        pieces += [fibres[6 * m : 6 * m + 6], gap]
    fibres = jnp.concatenate(pieces, 0).astype(jnp.bfloat16)
    square_ref[...] = jnp.zeros(square_ref.shape, jnp.float32)
    square_ref[0:6, 0:6] = matrix_ref[...]
    turned = transposed_lanes(square_ref[...])
    matrix = jnp.concatenate(
        [jnp.broadcast_to(turned[0:8, m : m + 1], (8, LANES)) for m in range(6)], 0
    )
    chunk = 1024
    for i, start in enumerate(range(0, weights_ref.shape[0], chunk)):
        if copies:
            copies[i].wait()
        parts = []
        for group in range(CLASSES):
            columns = slice(LANES * group, LANES * (group + 1))
            parts.append(
                lax.dot_general(
                    fibres[:, columns],
                    weights_ref[pl.ds(start, chunk), columns],
                    NT,
                    preferred_element_type=jnp.float32,
                )
            )
        for block in range(chunk // LANES):
            lanes = slice(LANES * block, LANES * (block + 1))
            level = class_ref[pl.ds((first + start) // LANES + block, 1), :]
            total = parts[0][:, lanes]
            for group in range(1, CLASSES):
                total = total + jnp.where(level >= group, parts[group][:, lanes], 0.0)
            scale = 1.0 / ((level + 1) * LANES).astype(jnp.float32)
            out_ref[:, pl.ds(start + LANES * block, LANES)] = total * scale + matrix


def fields_first(packed_ref, width):
    rows = packed_ref.shape[0] // width
    return halves(
        jnp.concatenate([packed_ref[pl.ds(f, rows, stride=width), :] for f in range(6)], 0)
    )


def respond_kernel(
    arrived_ref, early_ref, late_ref, out_ref, member_ref, lows_ref, answer_ref
):
    owners = arrived_ref.shape[0] // 7
    half = early_ref.shape[1] // LANES
    blocks = 2 * half
    rows = iota((blocks, LANES), 0)
    lane = (iota((blocks, LANES), 1) + 1).astype(jnp.float32)
    slots = []
    for sender in range(owners):
        slot = arrived_ref[pl.ds(7 * sender + 6, 1), :].astype(jnp.int32) - 1
        slots.append(slot)
        named = rows == (slot >> 7)
        columns = pl.ds(sender * LANES, LANES)
        member_ref[pl.ds(0, blocks), columns] = jnp.where(named, float(sender), 0.0).astype(
            jnp.bfloat16
        )
        member_ref[pl.ds(blocks, blocks), columns] = jnp.where(named, lane, 0.0).astype(jnp.bfloat16)
        lows_ref[:, columns] = one_hot(slot & (LANES - 1))
    where = lax.dot_general(
        member_ref[...], lows_ref[...], NT, preferred_element_type=jnp.float32
    ).astype(jnp.int32)

    table = fields_first(arrived_ref, 7)
    for block in range(0, blocks, STEP):
        steps = range(block, block + STEP)
        columns = jnp.concatenate([one_hot(where[blocks + b : blocks + b + 1] - 1) for b in steps], 1)
        found = looked_up(table, 6, [spread(where[b : b + 1]) for b in steps], columns)
        for i, b in enumerate(steps):
            tangent_ref = early_ref if b < half else late_ref
            lanes = pl.ds(b % half * LANES, LANES)
            total = jnp.zeros((8, LANES), jnp.float32)
            for m in range(6):
                total = total + tangent_ref[pl.ds(8 * m, 8), lanes] * found[i][m]
            answer_ref[pl.ds(8 * b, 8), :] = total

    table = fields_first(answer_ref, 8)
    for sender in range(0, owners, STEP):
        columns = lows_ref[:, pl.ds(sender * LANES, STEP * LANES)]
        highs = [spread(slot >> 7) for slot in slots[sender : sender + STEP]]
        for i, found in enumerate(looked_up(table, 6, highs, columns)):
            out_ref[pl.ds(6 * (sender + i), 6), :] = stacked(found)[0:6]


def faces_kernel(
    width_x, returned_ref, helper_ref, rank_ref, edge_ref, side_ref, end_ref, last_ref
):
    blocks = helper_ref.shape[0]
    table = fields_first(returned_ref, 6)
    edge = edge_ref[0:2].astype(jnp.int32)
    plane = list(range(blocks - 8, blocks))
    for group in (plane[:4], plane[4:], list(range(7, blocks - 8, 8)) + [blocks]):
        highs, lows = [], []
        for b in group:
            highs.append(spread(helper_ref[pl.ds(b, 1), :] if b < blocks else edge[0:1]))
            lows.append(one_hot(rank_ref[pl.ds(b, 1), :] if b < blocks else edge_ref[1:2]))
        values = looked_up(table, 6, highs, jnp.concatenate(lows, 1))
        for b, found in zip(group, values):
            for f in range(6):
                row = found[f][0:1]
                if b == blocks:
                    continue
                if b >= blocks - 8:
                    side_ref[pl.ds(8 * f + b - blocks + 8, 1), :] = row
                if b % 8 == 7:
                    end_ref[pl.ds(width_x * f + b // 8, 1), :] = row
            if b == blocks:
                part = iota((8, LANES), 1) // blocks
                for half in range(2):
                    row = jnp.zeros((8, LANES), jnp.float32)
                    for g in range(3):
                        row = jnp.where(part == g, found[3 * half + g], row)
                    last_ref[pl.ds(half, 1), :] = row[0:1]
    last_ref[pl.ds(2, 6), :] = jnp.zeros((6, LANES), jnp.float32)


def collect_kernel(returned_ref, helper_ref, rank_ref, sens_ref):
    blocks = helper_ref.shape[0]
    table = fields_first(returned_ref, 6)
    for block in range(0, blocks, STEP):
        steps = range(block, block + STEP)
        highs = [spread(helper_ref[pl.ds(b, 1), :]) for b in steps]
        columns = jnp.concatenate([one_hot(rank_ref[pl.ds(b, 1), :]) for b in steps], 1)
        for i, found in enumerate(looked_up(table, 6, highs, columns)):
            for f in range(6):
                sens_ref[pl.ds(blocks * f + block + i, 1), :] = found[f][0:1]


def force_kernel(width_x, inside_ref, sens_ref, last_ref, side_ref, corner_ref, prior_ref, out_ref):
    planes = width_x
    blocks = 8 * planes
    fields = 6
    in_x, in_y, in_z = (inside_ref[i] != 0 for i in range(3, 6))
    rows = jnp.concatenate(
        [
            last_ref[0:2],
            side_ref[54:56],
            corner_ref[0:2],
            side_ref[56:58],
        ],
        0,
    )
    edges = transposed_lanes(rows)
    sums = {}
    for f in range(fields):
        for x in range(-1, planes):
            part, g = f // 3, f % 3
            if x >= 0:
                here = sens_ref[pl.ds(blocks * f + 8 * x, 8), :]
                above = prior_ref[pl.ds(planes * f + x, 1), :]
                spot, column = blocks * g + 8 * x, part
            else:
                here = side_ref[pl.ds(8 * f, 8), :]
                above = side_ref[pl.ds(8 * fields + f, 1), :]
                spot, column = blocks * g + 8 * (planes - 1), part + 2
            edge = jnp.where(in_z, edges[spot : spot + 8, column : column + 1], 0.0)
            corner = jnp.where(in_z, edges[spot + 7 : spot + 8, column + 4 : column + 5], 0.0)
            if x < 0:
                here, edge = jnp.where(in_x, here, 0.0), jnp.where(in_x, edge, 0.0)
                above, corner = jnp.where(in_x, above, 0.0), jnp.where(in_x, corner, 0.0)
            above, corner = jnp.where(in_y, above, 0.0), jnp.where(in_y, corner, 0.0)
            here_z = jnp.concatenate([edge, here[:, :-1]], 1)
            there = jnp.concatenate([above, here[:-1]], 0)
            there_z = jnp.concatenate([jnp.concatenate([corner, above[:, :-1]], 1), here_z[:-1]], 0)
            low, high = there + there_z, here + here_z
            sums[f, x] = (low + high, low - high, (here_z - here) + (there_z - there))

    def both(f, x, kind):
        return sums[f, x][kind] + sums[f, x - 1][kind]

    def jump(f, x):
        return sums[f, x - 1][0] - sums[f, x][0]

    along = ((0, 5, 4), (5, 1, 3), (4, 3, 2))
    for d in range(3):
        for x in range(planes):
            force = jump(along[d][0], x) + both(along[d][1], x, 1) + both(along[d][2], x, 2)
            out_ref[pl.ds(blocks * d + 8 * x, 8), :] = 0.25 * force


def per_device(
    adjoint_disp, matrix_tangent, fibre_blocks, fibre_weights, rve_class, rve_helper, rve_slot
):
    owners = lax.axis_size("gx") * lax.axis_size("gy")
    width_x, width_y, width_z = adjoint_disp.shape[1:]
    points = width_x * width_y * width_z
    blocks = points // LANES
    fibres = fibre_weights.shape[1]
    places = [lax.axis_index(axis) for axis in ("gx", "gy", "gz")]
    ends = [lax.axis_size(axis) - 1 for axis in ("gx", "gy", "gz")]
    inside = jnp.stack(
        [place < end for place, end in zip(places, ends)] + [place > 0 for place in places]
    ).astype(jnp.int32)

    with jax.named_scope("fetch"):
        inputs = (
            adjoint_disp.reshape(3 * blocks, LANES),
            rve_helper.reshape(blocks, LANES),
            rve_slot.reshape(blocks, LANES),
            rve_class.reshape(blocks, LANES),
            fibre_blocks,
            matrix_tangent,
        )
        kept = [jax.ShapeDtypeStruct(a.shape, a.dtype) for a in inputs]
        first, disp, helper, slot, level, fibre, matrix = whole_call(
            functools.partial(fetch_kernel, len(inputs)),
            "fetch",
            [f32(8, LANES)] + kept,
            [pltpu.with_memory_space_constraint(a, pltpu.HBM) for a in inputs],
            [pltpu.SemaphoreType.DMA((len(inputs),))],
            places=[HBM] * len(inputs),
        )
        disp_grid = disp.reshape(3, width_x, width_y, LANES)

    with jax.named_scope("route"):
        weights_hbm = pltpu.with_memory_space_constraint(fibre_weights, pltpu.HBM)
        high, low, rank, edge, weights = whole_call(
            functools.partial(route_kernel, owners),
            "route",
            [
                i32(owners, LANES),
                jax.ShapeDtypeStruct((LANES, owners * LANES), jnp.bfloat16),
                f32(blocks, LANES),
                f32(8, LANES),
                jax.ShapeDtypeStruct((points // 2, fibres), fibre_weights.dtype),
            ],
            (helper, weights_hbm),
            [
                pltpu.VMEM((2 * owners, points), jnp.bfloat16),
                pltpu.VMEM((LANES, points), jnp.bfloat16),
                pltpu.SemaphoreType.DMA(()),
            ],
            flops=2 * points * LANES * 2 * owners,
            places=[VMEM, HBM],
        )

    with jax.named_scope("tangent"):
        half = points // 2
        early = whole_call(
            functools.partial(tangent_kernel, 0),
            "early_tangent",
            f32(48, half),
            (weights, level, fibre, matrix),
            [pltpu.VMEM((8, LANES), jnp.float32)],
            flops=256 * points * fibres,
        )
        late = whole_call(
            functools.partial(fetched_tangent_kernel, half),
            "late_tangent",
            f32(48, half),
            (weights_hbm, level, fibre, matrix),
            [
                pltpu.VMEM((8, LANES), jnp.float32),
                pltpu.VMEM((half, fibres), jnp.bfloat16),
                pltpu.SemaphoreType.DMA((2,)),
            ],
            flops=256 * points * fibres,
            places=[HBM, VMEM, VMEM, VMEM],
        )

    with jax.named_scope("lift"):
        side = passed_round(disp_grid[:, 0].reshape(24, LANES), ("gx",), -1)
        corner = passed_round(first, ("gx", "gz"), -1)
        first = passed_round(first, ("gz",), -1)
        side, corner, first, high, low, rank, edge, early, inside = lax.optimization_barrier(
            (side, corner, first, high, low, rank, edge, early, inside)
        )
        next_y = jnp.concatenate(
            [
                disp_grid[:, :, 0].reshape(3 * width_x, LANES),
                side[0:24:8],
                first[0:1],
                corner[0:1],
            ],
            0,
        )
        next_y = passed_round(next_y, ("gy",), -1)
        next_y, late = lax.optimization_barrier((next_y, late))

    with jax.named_scope("strain"):
        buckets = whole_call(
            functools.partial(strain_kernel, owners, width_x),
            "strain",
            f32(owners * 7, LANES),
            (inside, disp, first, side, corner, next_y, high, low, slot),
            [pltpu.VMEM((7 * blocks, LANES), jnp.float32)],
            places=[SMEM] + [VMEM] * 8,
        )

    with jax.named_scope("exchange"):
        arrived = exchanged(buckets, owners, ("gx", "gy"))

    with jax.named_scope("respond"):
        answer = whole_call(
            respond_kernel,
            "respond",
            f32(owners * 6, LANES),
            (arrived, early, late),
            [
                pltpu.VMEM((2 * blocks, owners * LANES), jnp.bfloat16),
                pltpu.VMEM((LANES, owners * LANES), jnp.bfloat16),
                pltpu.VMEM((8 * blocks, LANES), jnp.float32),
            ],
        )

    with jax.named_scope("return"):
        returned = exchanged(answer, owners, ("gx", "gy"))

    with jax.named_scope("collect"):
        side, end, last = whole_call(
            functools.partial(faces_kernel, width_x),
            "faces",
            [f32(48, LANES), f32(6 * width_x, LANES), f32(8, LANES)],
            (returned, helper, rank, edge),
        )
        sens = whole_call(
            collect_kernel,
            "collect",
            f32(6 * blocks, LANES),
            (returned, helper, rank),
        )

    with jax.named_scope("settle"):
        prior = passed_round(end, ("gy",), 1)
        corner = passed_on(last, ("gy", "gz"), 1)
        last = passed_round(last, ("gz",), 1)
        side = jnp.concatenate(
            [side, prior[width_x - 1 : 6 * width_x : width_x], last[0:2], corner[0:2]], 0
        )
        side = passed_on(side, ("gx",), 1)
        side, sens = lax.optimization_barrier((side, sens))
        force = whole_call(
            functools.partial(force_kernel, width_x),
            "force",
            f32(3 * blocks, LANES),
            (inside, sens, last, side, corner, prior),
            places=[SMEM] + [VMEM] * 5,
        )
    return force.reshape(3, width_x, width_y, width_z)


def solution(mesh):
    in_specs = (
        P(None, "gx", "gy", "gz"),
        P(),
        P(),
        P(("gx", "gy", "gz"), None),
        P(("gx", "gy", "gz")),
        P("gx", "gy", "gz"),
        P("gx", "gy", "gz"),
    )
    out_specs = P(None, "gx", "gy", "gz")
    return jax.shard_map(
        per_device, mesh=mesh, in_specs=in_specs, out_specs=out_specs, check_vma=False
    )
```

```python
import functools

import jax
import jax.numpy as jnp
from jax import lax
from jax.experimental import pallas as pl
from jax.experimental.pallas import tpu as pltpu
from jax.sharding import PartitionSpec as P

CLASSES = 4
LANES = 128
STEP = 4
SMEM = pl.BlockSpec(memory_space=pltpu.SMEM)
HBM = pl.BlockSpec(memory_space=pltpu.HBM)
VMEM = pl.BlockSpec(memory_space=pltpu.VMEM)
NT = (((1,), (1,)), ((), ()))


def passed_round(array, axes, by):
    pairs = [(0, 0)]
    for axis in axes:
        size = lax.axis_size(axis)
        pairs = [
            (source * size + i, target * size + (i + by) % size)
            for source, target in pairs
            for i in range(size)
        ]
    return lax.ppermute(array, axes, pairs)


def passed_on(array, axes, by):
    pairs = [(0, 0)]
    for axis in axes:
        size = lax.axis_size(axis)
        pairs = [
            (source * size + i, target * size + i + by)
            for source, target in pairs
            for i in range(size)
            if 0 <= i + by < size
        ]
    return lax.ppermute(array, axes, pairs)


def exchanged(array, owners, axes):
    flat = array.reshape(owners, 1, -1)
    flat = lax.all_to_all(flat, axes, split_axis=0, concat_axis=0, tiled=True)
    return flat.reshape(array.shape)


def whole_call(kernel, name, out, inputs, scratch=(), flops=0, places=None):
    return pl.pallas_call(
        kernel,
        name=name,
        out_shape=out,
        in_specs=places or [VMEM] * len(inputs),
        out_specs=[VMEM] * len(out) if isinstance(out, (list, tuple)) else VMEM,
        scratch_shapes=list(scratch),
        cost_estimate=pl.CostEstimate(flops=flops, bytes_accessed=1 << 20, transcendentals=0),
        compiler_params=pltpu.CompilerParams(vmem_limit_bytes=16 << 20),
    )(*inputs)


def f32(*shape):
    return jax.ShapeDtypeStruct(shape, jnp.float32)


def i32(*shape):
    return jax.ShapeDtypeStruct(shape, jnp.int32)


def iota(shape, dim):
    return lax.broadcasted_iota(jnp.int32, shape, dim)


def halves(table):
    high = table.astype(jnp.bfloat16)
    low = (table - high.astype(jnp.float32)).astype(jnp.bfloat16)
    return jnp.concatenate([high, low], 1)


def one_hot(low):
    place = iota((LANES, LANES), 0).astype(jnp.float32).astype(jnp.bfloat16)
    low = jnp.broadcast_to(low.astype(jnp.float32).astype(jnp.bfloat16), (LANES, LANES))
    return jnp.where(place == low, jnp.ones((), jnp.bfloat16), jnp.zeros((), jnp.bfloat16))


def looked_up(table, fields, highs, columns):
    products = jnp.dot(
        table, jnp.concatenate([columns, columns], 0), preferred_element_type=jnp.float32
    )
    rows = table.shape[0] // fields
    place = iota((8, LANES), 0)
    found = []
    for i, high in enumerate(highs):
        lanes = slice(LANES * i, LANES * (i + 1))
        named = [place == high - 8 * g for g in range(rows // 8)]
        values = []
        for f in range(fields):
            total = jnp.zeros((8, LANES), jnp.float32)
            for g, here in enumerate(named):
                start = rows * f + 8 * g
                total = jnp.where(here, products[start : start + 8, lanes], total)
            for shift in (4, 2, 1):
                total = total + pltpu.roll(total, shift, 0)
            values.append(total)
        found.append(values)
    return found


def stacked(values):
    place = iota((8, LANES), 0)
    tile = values[0]
    for f in range(1, len(values)):
        tile = jnp.where(place == f, values[f], tile)
    return tile


def spread(row):
    return jnp.broadcast_to(row, (8, LANES))


def transposed_lanes(block):
    gap = LANES - block.shape[0]
    if gap:
        block = jnp.concatenate([block, jnp.zeros((gap, LANES), block.dtype)], 0)
    return block.T


def fetch_kernel(count, *refs):
    inputs, (first_ref, *kept, sems) = refs[:count], refs[count:]
    copies = [
        pltpu.make_async_copy(source, target, sems.at[i])
        for i, (source, target) in enumerate(zip(inputs, kept))
    ]
    for copy in copies:
        copy.start()
    copies[0].wait()
    first_ref[...] = transposed_lanes(kept[0][...])[0:8]
    for copy in copies[1:]:
        copy.wait()


def last_lanes(block):
    tile = transposed_lanes(block)[LANES - 8 :]
    rows = block.shape[0]
    return (tile + pltpu.roll(tile, rows, 1) + pltpu.roll(tile, 2 * rows, 1))[7:8]


def route_kernel(
    owners,
    helper_ref,
    weights_hbm,
    high_ref,
    low_ref,
    rank_ref,
    edge_ref,
    weights_ref,
    member_ref,
    ranks_ref,
    sem,
):
    copy = pltpu.make_async_copy(weights_hbm.at[pl.ds(0, weights_ref.shape[0])], weights_ref, sem)
    copy.start()
    blocks = helper_ref.shape[0]
    upper = (iota((LANES, 2 * LANES), 0) <= iota((LANES, 2 * LANES), 1)).astype(jnp.bfloat16)
    owner = iota((owners, LANES), 0)
    lane = iota((owners, LANES), 1)
    before = jnp.zeros((owners, LANES), jnp.float32)
    for block in range(blocks):
        member = helper_ref[pl.ds(block, 1), :] == owner
        counted = jnp.dot(
            jnp.where(member, 1.0, 0.0).astype(jnp.bfloat16),
            upper,
            preferred_element_type=jnp.float32,
        )
        rank = before + counted[:, :LANES] - 1.0
        rank = jnp.sum(jnp.where(member, rank, 0.0), 0, keepdims=True)
        before = before + counted[:, LANES:]
        columns = pl.ds(block * LANES, LANES)
        member_ref[pl.ds(0, owners), columns] = jnp.where(member, float(block), 0.0).astype(
            jnp.bfloat16
        )
        member_ref[pl.ds(owners, owners), columns] = jnp.where(
            member, (lane + 1).astype(jnp.float32), 0.0
        ).astype(jnp.bfloat16)
        rank_ref[pl.ds(block, 1), :] = rank
        ranks_ref[:, columns] = one_hot(rank)
    found = lax.dot_general(
        member_ref[...], ranks_ref[...], NT, preferred_element_type=jnp.float32
    ).astype(jnp.int32)
    lows = found[owners:] - 1
    high_ref[...] = jnp.where(lows < 0, -1, found[:owners])
    for bucket in range(owners):
        low_ref[:, pl.ds(bucket * LANES, LANES)] = one_hot(lows[bucket : bucket + 1])
    edge_ref[...] = jnp.concatenate(
        [
            last_lanes(helper_ref[...].astype(jnp.float32)),
            last_lanes(rank_ref[...]),
            jnp.zeros((6, LANES), jnp.float32),
        ],
        0,
    )
    copy.wait()


def strain_kernel(
    owners,
    width_x,
    inside_ref,
    disp_ref,
    first_ref,
    side_ref,
    corner_ref,
    next_ref,
    high_ref,
    low_ref,
    slot_ref,
    out_ref,
    field_ref,
):
    planes = width_x
    in_x, in_y, in_z = (inside_ref[i] != 0 for i in range(3))
    edges = transposed_lanes(
        jnp.concatenate(
            [
                first_ref[0:1],
                corner_ref[0:1],
                next_ref[15:16],
                next_ref[16:17],
                jnp.zeros((4, LANES), jnp.float32),
            ],
            0,
        )
    )
    sums = {}
    for c in range(3):
        for x in range(planes + 1):
            k = c * planes + x
            if x < planes:
                here = disp_ref[pl.ds(8 * k, 8), :]
                above = next_ref[pl.ds(k, 1), :]
                spot, column = 8 * k, 0
            else:
                here = side_ref[pl.ds(8 * c, 8), :]
                above = next_ref[pl.ds(3 * planes + c, 1), :]
                spot, column = 8 * c * planes, 1
            edge = jnp.where(in_z, edges[spot : spot + 8, column : column + 1], 0.0)
            corner = jnp.where(in_z, edges[spot : spot + 1, column + 2 : column + 3], 0.0)
            if x == planes:
                here, edge = jnp.where(in_x, here, 0.0), jnp.where(in_x, edge, 0.0)
                above, corner = jnp.where(in_x, above, 0.0), jnp.where(in_x, corner, 0.0)
            above, corner = jnp.where(in_y, above, 0.0), jnp.where(in_y, corner, 0.0)
            here_z = jnp.concatenate([here[:, 1:], edge], 1)
            there = jnp.concatenate([here[1:], above], 0)
            there_z = jnp.concatenate([here_z[1:], jnp.concatenate([above[:, 1:], corner], 1)], 0)
            low, high = here + here_z, there + there_z
            sums[c, x] = (low + high, high - low, (here_z - here) + (there_z - there))
    for x in range(planes):
        grad_x = [0.25 * (sums[c, x + 1][0] - sums[c, x][0]) for c in range(3)]
        grad_y = [0.25 * (sums[c, x + 1][1] + sums[c, x][1]) for c in range(3)]
        grad_z = [0.25 * (sums[c, x + 1][2] + sums[c, x][2]) for c in range(3)]
        slot = (slot_ref[pl.ds(8 * x, 8), :] + 1).astype(jnp.float32)
        fields = (
            grad_x[0],
            grad_y[1],
            grad_z[2],
            grad_z[1] + grad_y[2],
            grad_z[0] + grad_x[2],
            grad_y[0] + grad_x[1],
            slot,
        )
        for f, field in enumerate(fields):
            field_ref[pl.ds(8 * (planes * f + x), 8), :] = field
    table = halves(field_ref[...])
    for owner in range(0, owners, STEP):
        steps = range(owner, owner + STEP)
        highs = [spread(high_ref[pl.ds(o, 1), :]) for o in steps]
        columns = low_ref[:, pl.ds(owner * LANES, STEP * LANES)]
        for o, found in zip(steps, looked_up(table, 7, highs, columns)):
            out_ref[pl.ds(7 * o, 7), :] = stacked(found)[0:7]


def tangent_kernel(first, weights_ref, class_ref, blocks_ref, matrix_ref, out_ref, square_ref):
    tangents(first, weights_ref, [], class_ref, blocks_ref, matrix_ref, out_ref, square_ref)


def fetched_tangent_kernel(
    first, weights_hbm, class_ref, blocks_ref, matrix_ref, out_ref, square_ref, weights_ref, sems
):
    chunk = weights_ref.shape[0] // sems.shape[0]
    copies = [
        pltpu.make_async_copy(
            weights_hbm.at[pl.ds(first + chunk * i, chunk)],
            weights_ref.at[pl.ds(chunk * i, chunk)],
            sems.at[i],
        )
        for i in range(sems.shape[0])
    ]
    for copy in copies:
        copy.start()
    tangents(first, weights_ref, copies, class_ref, blocks_ref, matrix_ref, out_ref, square_ref)


def tangents(first, weights_ref, copies, class_ref, blocks_ref, matrix_ref, out_ref, square_ref):
    fibres = blocks_ref[...].astype(jnp.float32)
    gap = jnp.zeros((2, fibres.shape[1]), jnp.float32)
    pieces = []
    for m in range(6):
        pieces += [fibres[6 * m : 6 * m + 6], gap]
    fibres = jnp.concatenate(pieces, 0).astype(jnp.bfloat16)
    square_ref[...] = jnp.zeros(square_ref.shape, jnp.float32)
    square_ref[0:6, 0:6] = matrix_ref[...]
    turned = transposed_lanes(square_ref[...])
    matrix = jnp.concatenate(
        [jnp.broadcast_to(turned[0:8, m : m + 1], (8, LANES)) for m in range(6)], 0
    )
    chunk = 1024
    for i, start in enumerate(range(0, weights_ref.shape[0], chunk)):
        if copies:
            copies[i].wait()
        parts = []
        for group in range(CLASSES):
            columns = slice(LANES * group, LANES * (group + 1))
            parts.append(
                lax.dot_general(
                    fibres[:, columns],
                    weights_ref[pl.ds(start, chunk), columns],
                    NT,
                    preferred_element_type=jnp.float32,
                )
            )
        for block in range(chunk // LANES):
            lanes = slice(LANES * block, LANES * (block + 1))
            level = class_ref[pl.ds((first + start) // LANES + block, 1), :]
            total = parts[0][:, lanes]
            for group in range(1, CLASSES):
                total = total + jnp.where(level >= group, parts[group][:, lanes], 0.0)
            scale = 1.0 / ((level + 1) * LANES).astype(jnp.float32)
            out_ref[:, pl.ds(start + LANES * block, LANES)] = total * scale + matrix


def fields_first(packed_ref, width):
    rows = packed_ref.shape[0] // width
    return halves(
        jnp.concatenate([packed_ref[pl.ds(f, rows, stride=width), :] for f in range(6)], 0)
    )


def respond_kernel(
    arrived_ref, early_ref, late_ref, out_ref, member_ref, lows_ref, answer_ref
):
    owners = arrived_ref.shape[0] // 7
    half = early_ref.shape[1] // LANES
    blocks = 2 * half
    rows = iota((blocks, LANES), 0)
    lane = (iota((blocks, LANES), 1) + 1).astype(jnp.float32)
    slots = []
    for sender in range(owners):
        slot = arrived_ref[pl.ds(7 * sender + 6, 1), :].astype(jnp.int32) - 1
        slots.append(slot)
        named = rows == (slot >> 7)
        columns = pl.ds(sender * LANES, LANES)
        member_ref[pl.ds(0, blocks), columns] = jnp.where(named, float(sender), 0.0).astype(
            jnp.bfloat16
        )
        member_ref[pl.ds(blocks, blocks), columns] = jnp.where(named, lane, 0.0).astype(jnp.bfloat16)
        lows_ref[:, columns] = one_hot(slot & (LANES - 1))
    where = lax.dot_general(
        member_ref[...], lows_ref[...], NT, preferred_element_type=jnp.float32
    ).astype(jnp.int32)

    table = fields_first(arrived_ref, 7)
    for block in range(0, blocks, STEP):
        steps = range(block, block + STEP)
        columns = jnp.concatenate([one_hot(where[blocks + b : blocks + b + 1] - 1) for b in steps], 1)
        found = looked_up(table, 6, [spread(where[b : b + 1]) for b in steps], columns)
        for i, b in enumerate(steps):
            tangent_ref = early_ref if b < half else late_ref
            lanes = pl.ds(b % half * LANES, LANES)
            total = jnp.zeros((8, LANES), jnp.float32)
            for m in range(6):
                total = total + tangent_ref[pl.ds(8 * m, 8), lanes] * found[i][m]
            answer_ref[pl.ds(8 * b, 8), :] = total

    table = fields_first(answer_ref, 8)
    for sender in range(0, owners, STEP):
        columns = lows_ref[:, pl.ds(sender * LANES, STEP * LANES)]
        highs = [spread(slot >> 7) for slot in slots[sender : sender + STEP]]
        for i, found in enumerate(looked_up(table, 6, highs, columns)):
            out_ref[pl.ds(6 * (sender + i), 6), :] = stacked(found)[0:6]


def faces_kernel(
    width_x, returned_ref, helper_ref, rank_ref, edge_ref, side_ref, end_ref, last_ref
):
    blocks = helper_ref.shape[0]
    table = fields_first(returned_ref, 6)
    edge = edge_ref[0:2].astype(jnp.int32)
    plane = list(range(blocks - 8, blocks))
    for group in (plane[:4], plane[4:], list(range(7, blocks - 8, 8)) + [blocks]):
        highs, lows = [], []
        for b in group:
            highs.append(spread(helper_ref[pl.ds(b, 1), :] if b < blocks else edge[0:1]))
            lows.append(one_hot(rank_ref[pl.ds(b, 1), :] if b < blocks else edge_ref[1:2]))
        values = looked_up(table, 6, highs, jnp.concatenate(lows, 1))
        for b, found in zip(group, values):
            for f in range(6):
                row = found[f][0:1]
                if b == blocks:
                    continue
                if b >= blocks - 8:
                    side_ref[pl.ds(8 * f + b - blocks + 8, 1), :] = row
                if b % 8 == 7:
                    end_ref[pl.ds(width_x * f + b // 8, 1), :] = row
            if b == blocks:
                part = iota((8, LANES), 1) // blocks
                for half in range(2):
                    row = jnp.zeros((8, LANES), jnp.float32)
                    for g in range(3):
                        row = jnp.where(part == g, found[3 * half + g], row)
                    last_ref[pl.ds(half, 1), :] = row[0:1]
    last_ref[pl.ds(2, 6), :] = jnp.zeros((6, LANES), jnp.float32)


def collect_kernel(returned_ref, helper_ref, rank_ref, sens_ref):
    blocks = helper_ref.shape[0]
    table = fields_first(returned_ref, 6)
    for block in range(0, blocks, STEP):
        steps = range(block, block + STEP)
        highs = [spread(helper_ref[pl.ds(b, 1), :]) for b in steps]
        columns = jnp.concatenate([one_hot(rank_ref[pl.ds(b, 1), :]) for b in steps], 1)
        for i, found in enumerate(looked_up(table, 6, highs, columns)):
            for f in range(6):
                sens_ref[pl.ds(blocks * f + block + i, 1), :] = found[f][0:1]


def force_kernel(width_x, inside_ref, sens_ref, last_ref, side_ref, corner_ref, prior_ref, out_ref):
    planes = width_x
    blocks = 8 * planes
    fields = 6
    in_x, in_y, in_z = (inside_ref[i] != 0 for i in range(3, 6))
    rows = jnp.concatenate(
        [
            last_ref[0:2],
            side_ref[54:56],
            corner_ref[0:2],
            side_ref[56:58],
        ],
        0,
    )
    edges = transposed_lanes(rows)
    sums = {}
    for f in range(fields):
        for x in range(-1, planes):
            part, g = f // 3, f % 3
            if x >= 0:
                here = sens_ref[pl.ds(blocks * f + 8 * x, 8), :]
                above = prior_ref[pl.ds(planes * f + x, 1), :]
                spot, column = blocks * g + 8 * x, part
            else:
                here = side_ref[pl.ds(8 * f, 8), :]
                above = side_ref[pl.ds(8 * fields + f, 1), :]
                spot, column = blocks * g + 8 * (planes - 1), part + 2
            edge = jnp.where(in_z, edges[spot : spot + 8, column : column + 1], 0.0)
            corner = jnp.where(in_z, edges[spot + 7 : spot + 8, column + 4 : column + 5], 0.0)
            if x < 0:
                here, edge = jnp.where(in_x, here, 0.0), jnp.where(in_x, edge, 0.0)
                above, corner = jnp.where(in_x, above, 0.0), jnp.where(in_x, corner, 0.0)
            above, corner = jnp.where(in_y, above, 0.0), jnp.where(in_y, corner, 0.0)
            here_z = jnp.concatenate([edge, here[:, :-1]], 1)
            there = jnp.concatenate([above, here[:-1]], 0)
            there_z = jnp.concatenate([jnp.concatenate([corner, above[:, :-1]], 1), here_z[:-1]], 0)
            low, high = there + there_z, here + here_z
            sums[f, x] = (low + high, low - high, (here_z - here) + (there_z - there))

    def both(f, x, kind):
        return sums[f, x][kind] + sums[f, x - 1][kind]

    def jump(f, x):
        return sums[f, x - 1][0] - sums[f, x][0]

    along = ((0, 5, 4), (5, 1, 3), (4, 3, 2))
    for d in range(3):
        for x in range(planes):
            force = jump(along[d][0], x) + both(along[d][1], x, 1) + both(along[d][2], x, 2)
            out_ref[pl.ds(blocks * d + 8 * x, 8), :] = 0.25 * force


def per_device(
    adjoint_disp, matrix_tangent, fibre_blocks, fibre_weights, rve_class, rve_helper, rve_slot
):
    owners = lax.axis_size("gx") * lax.axis_size("gy")
    width_x, width_y, width_z = adjoint_disp.shape[1:]
    points = width_x * width_y * width_z
    blocks = points // LANES
    fibres = fibre_weights.shape[1]
    places = [lax.axis_index(axis) for axis in ("gx", "gy", "gz")]
    ends = [lax.axis_size(axis) - 1 for axis in ("gx", "gy", "gz")]
    inside = jnp.stack(
        [place < end for place, end in zip(places, ends)] + [place > 0 for place in places]
    ).astype(jnp.int32)

    with jax.named_scope("fetch"):
        inputs = (
            adjoint_disp.reshape(3 * blocks, LANES),
            rve_helper.reshape(blocks, LANES),
            rve_slot.reshape(blocks, LANES),
            rve_class.reshape(blocks, LANES),
            matrix_tangent,
        )
        kept = [jax.ShapeDtypeStruct(a.shape, a.dtype) for a in inputs]
        first, disp, helper, slot, level, matrix = whole_call(
            functools.partial(fetch_kernel, len(inputs)),
            "fetch",
            [f32(8, LANES)] + kept,
            [pltpu.with_memory_space_constraint(a, pltpu.HBM) for a in inputs],
            [pltpu.SemaphoreType.DMA((len(inputs),))],
            places=[HBM] * len(inputs),
        )
        disp_grid = disp.reshape(3, width_x, width_y, LANES)

    with jax.named_scope("route"):
        weights_hbm = pltpu.with_memory_space_constraint(fibre_weights, pltpu.HBM)
        high, low, rank, edge, weights = whole_call(
            functools.partial(route_kernel, owners),
            "route",
            [
                i32(owners, LANES),
                jax.ShapeDtypeStruct((LANES, owners * LANES), jnp.bfloat16),
                f32(blocks, LANES),
                f32(8, LANES),
                jax.ShapeDtypeStruct((points // 2, fibres), fibre_weights.dtype),
            ],
            (helper, weights_hbm),
            [
                pltpu.VMEM((2 * owners, points), jnp.bfloat16),
                pltpu.VMEM((LANES, points), jnp.bfloat16),
                pltpu.SemaphoreType.DMA(()),
            ],
            flops=2 * points * LANES * 2 * owners,
            places=[VMEM, HBM],
        )

    with jax.named_scope("tangent"):
        half = points // 2
        early = whole_call(
            functools.partial(tangent_kernel, 0),
            "early_tangent",
            f32(48, half),
            (weights, level, fibre_blocks, matrix),
            [pltpu.VMEM((8, LANES), jnp.float32)],
            flops=256 * points * fibres,
        )
        late = whole_call(
            functools.partial(fetched_tangent_kernel, half),
            "late_tangent",
            f32(48, half),
            (weights_hbm, level, fibre_blocks, matrix),
            [
                pltpu.VMEM((8, LANES), jnp.float32),
                pltpu.VMEM((half, fibres), jnp.bfloat16),
                pltpu.SemaphoreType.DMA((2,)),
            ],
            flops=256 * points * fibres,
            places=[HBM, VMEM, VMEM, VMEM],
        )

    with jax.named_scope("lift"):
        side = passed_round(disp_grid[:, 0].reshape(24, LANES), ("gx",), -1)
        corner = passed_round(first, ("gx", "gz"), -1)
        first = passed_round(first, ("gz",), -1)
        side, corner, first, high, low, rank, edge, early, inside = lax.optimization_barrier(
            (side, corner, first, high, low, rank, edge, early, inside)
        )
        next_y = jnp.concatenate(
            [
                disp_grid[:, :, 0].reshape(3 * width_x, LANES),
                side[0:24:8],
                first[0:1],
                corner[0:1],
            ],
            0,
        )
        next_y = passed_round(next_y, ("gy",), -1)
        next_y, late = lax.optimization_barrier((next_y, late))

    with jax.named_scope("strain"):
        buckets = whole_call(
            functools.partial(strain_kernel, owners, width_x),
            "strain",
            f32(owners * 7, LANES),
            (inside, disp, first, side, corner, next_y, high, low, slot),
            [pltpu.VMEM((7 * blocks, LANES), jnp.float32)],
            places=[SMEM] + [VMEM] * 8,
        )

    with jax.named_scope("exchange"):
        arrived = exchanged(buckets, owners, ("gx", "gy"))

    with jax.named_scope("respond"):
        answer = whole_call(
            respond_kernel,
            "respond",
            f32(owners * 6, LANES),
            (arrived, early, late),
            [
                pltpu.VMEM((2 * blocks, owners * LANES), jnp.bfloat16),
                pltpu.VMEM((LANES, owners * LANES), jnp.bfloat16),
                pltpu.VMEM((8 * blocks, LANES), jnp.float32),
            ],
        )

    with jax.named_scope("return"):
        returned = exchanged(answer, owners, ("gx", "gy"))

    with jax.named_scope("collect"):
        side, end, last = whole_call(
            functools.partial(faces_kernel, width_x),
            "faces",
            [f32(48, LANES), f32(6 * width_x, LANES), f32(8, LANES)],
            (returned, helper, rank, edge),
        )
        sens = whole_call(
            collect_kernel,
            "collect",
            f32(6 * blocks, LANES),
            (returned, helper, rank),
        )

    with jax.named_scope("settle"):
        prior = passed_round(end, ("gy",), 1)
        corner = passed_on(last, ("gy", "gz"), 1)
        last = passed_round(last, ("gz",), 1)
        side = jnp.concatenate(
            [side, prior[width_x - 1 : 6 * width_x : width_x], last[0:2], corner[0:2]], 0
        )
        side = passed_on(side, ("gx",), 1)
        side, sens = lax.optimization_barrier((side, sens))
        force = whole_call(
            functools.partial(force_kernel, width_x),
            "force",
            f32(3 * blocks, LANES),
            (inside, sens, last, side, corner, prior),
            places=[SMEM] + [VMEM] * 5,
        )
    return force.reshape(3, width_x, width_y, width_z)


def solution(mesh):
    in_specs = (
        P(None, "gx", "gy", "gz"),
        P(),
        P(),
        P(("gx", "gy", "gz"), None),
        P(("gx", "gy", "gz")),
        P("gx", "gy", "gz"),
        P("gx", "gy", "gz"),
    )
    out_specs = P(None, "gx", "gy", "gz")
    return jax.shard_map(
        per_device, mesh=mesh, in_specs=in_specs, out_specs=out_specs, check_vma=False
    )
```

```python
import functools

import jax
import jax.numpy as jnp
from jax import lax
from jax.experimental import pallas as pl
from jax.experimental.pallas import tpu as pltpu
from jax.sharding import PartitionSpec as P

CLASSES = 4
LANES = 128
STEP = 4
SMEM = pl.BlockSpec(memory_space=pltpu.SMEM)
HBM = pl.BlockSpec(memory_space=pltpu.HBM)
VMEM = pl.BlockSpec(memory_space=pltpu.VMEM)
NT = (((1,), (1,)), ((), ()))


def passed_round(array, axes, by):
    pairs = [(0, 0)]
    for axis in axes:
        size = lax.axis_size(axis)
        pairs = [
            (source * size + i, target * size + (i + by) % size)
            for source, target in pairs
            for i in range(size)
        ]
    return lax.ppermute(array, axes, pairs)


def passed_on(array, axes, by):
    pairs = [(0, 0)]
    for axis in axes:
        size = lax.axis_size(axis)
        pairs = [
            (source * size + i, target * size + i + by)
            for source, target in pairs
            for i in range(size)
            if 0 <= i + by < size
        ]
    return lax.ppermute(array, axes, pairs)


def exchanged(array, owners, axes):
    flat = array.reshape(owners, 1, -1)
    flat = lax.all_to_all(flat, axes, split_axis=0, concat_axis=0, tiled=True)
    return flat.reshape(array.shape)


def whole_call(kernel, name, out, inputs, scratch=(), flops=0, places=None):
    return pl.pallas_call(
        kernel,
        name=name,
        out_shape=out,
        in_specs=places or [VMEM] * len(inputs),
        out_specs=[VMEM] * len(out) if isinstance(out, (list, tuple)) else VMEM,
        scratch_shapes=list(scratch),
        cost_estimate=pl.CostEstimate(flops=flops, bytes_accessed=1 << 20, transcendentals=0),
        compiler_params=pltpu.CompilerParams(vmem_limit_bytes=16 << 20),
    )(*inputs)


def f32(*shape):
    return jax.ShapeDtypeStruct(shape, jnp.float32)


def i32(*shape):
    return jax.ShapeDtypeStruct(shape, jnp.int32)


def iota(shape, dim):
    return lax.broadcasted_iota(jnp.int32, shape, dim)


def halves(table):
    high = table.astype(jnp.bfloat16)
    low = (table - high.astype(jnp.float32)).astype(jnp.bfloat16)
    return jnp.concatenate([high, low], 1)


def one_hot(low):
    place = iota((LANES, LANES), 0).astype(jnp.float32).astype(jnp.bfloat16)
    low = jnp.broadcast_to(low.astype(jnp.float32).astype(jnp.bfloat16), (LANES, LANES))
    return jnp.where(place == low, jnp.ones((), jnp.bfloat16), jnp.zeros((), jnp.bfloat16))


def looked_up(table, fields, highs, columns):
    products = jnp.dot(
        table, jnp.concatenate([columns, columns], 0), preferred_element_type=jnp.float32
    )
    rows = table.shape[0] // fields
    place = iota((8, LANES), 0)
    found = []
    for i, high in enumerate(highs):
        lanes = slice(LANES * i, LANES * (i + 1))
        named = [place == high - 8 * g for g in range(rows // 8)]
        values = []
        for f in range(fields):
            total = jnp.zeros((8, LANES), jnp.float32)
            for g, here in enumerate(named):
                start = rows * f + 8 * g
                total = jnp.where(here, products[start : start + 8, lanes], total)
            for shift in (4, 2, 1):
                total = total + pltpu.roll(total, shift, 0)
            values.append(total)
        found.append(values)
    return found


def stacked(values):
    place = iota((8, LANES), 0)
    tile = values[0]
    for f in range(1, len(values)):
        tile = jnp.where(place == f, values[f], tile)
    return tile


def spread(row):
    return jnp.broadcast_to(row, (8, LANES))


def transposed_lanes(block):
    gap = LANES - block.shape[0]
    if gap:
        block = jnp.concatenate([block, jnp.zeros((gap, LANES), block.dtype)], 0)
    return block.T


def fetch_kernel(count, *refs):
    inputs, (first_ref, *kept, sems) = refs[:count], refs[count:]
    copies = [
        pltpu.make_async_copy(source, target, sems.at[i])
        for i, (source, target) in enumerate(zip(inputs, kept))
    ]
    for copy in copies:
        copy.start()
    copies[0].wait()
    first_ref[...] = transposed_lanes(kept[0][...])[0:8]
    for copy in copies[1:]:
        copy.wait()


def last_lanes(block):
    tile = transposed_lanes(block)[LANES - 8 :]
    rows = block.shape[0]
    return (tile + pltpu.roll(tile, rows, 1) + pltpu.roll(tile, 2 * rows, 1))[7:8]


def route_kernel(
    owners,
    helper_ref,
    weights_hbm,
    high_ref,
    low_ref,
    rank_ref,
    edge_ref,
    weights_ref,
    member_ref,
    ranks_ref,
    sem,
):
    copy = pltpu.make_async_copy(weights_hbm.at[pl.ds(0, weights_ref.shape[0])], weights_ref, sem)
    copy.start()
    blocks = helper_ref.shape[0]
    upper = (iota((LANES, 2 * LANES), 0) <= iota((LANES, 2 * LANES), 1)).astype(jnp.bfloat16)
    owner = iota((owners, LANES), 0)
    lane = iota((owners, LANES), 1)
    before = jnp.zeros((owners, LANES), jnp.float32)
    for block in range(blocks):
        member = helper_ref[pl.ds(block, 1), :] == owner
        counted = jnp.dot(
            jnp.where(member, 1.0, 0.0).astype(jnp.bfloat16),
            upper,
            preferred_element_type=jnp.float32,
        )
        rank = before + counted[:, :LANES] - 1.0
        rank = jnp.sum(jnp.where(member, rank, 0.0), 0, keepdims=True)
        before = before + counted[:, LANES:]
        columns = pl.ds(block * LANES, LANES)
        member_ref[pl.ds(0, owners), columns] = jnp.where(member, float(block), 0.0).astype(
            jnp.bfloat16
        )
        member_ref[pl.ds(owners, owners), columns] = jnp.where(
            member, (lane + 1).astype(jnp.float32), 0.0
        ).astype(jnp.bfloat16)
        rank_ref[pl.ds(block, 1), :] = rank
        ranks_ref[:, columns] = one_hot(rank)
    found = lax.dot_general(
        member_ref[...], ranks_ref[...], NT, preferred_element_type=jnp.float32
    ).astype(jnp.int32)
    lows = found[owners:] - 1
    high_ref[...] = jnp.where(lows < 0, -1, found[:owners])
    for bucket in range(owners):
        low_ref[:, pl.ds(bucket * LANES, LANES)] = one_hot(lows[bucket : bucket + 1])
    edge_ref[...] = jnp.concatenate(
        [
            last_lanes(helper_ref[...].astype(jnp.float32)),
            last_lanes(rank_ref[...]),
            jnp.zeros((6, LANES), jnp.float32),
        ],
        0,
    )
    copy.wait()


def strain_kernel(
    owners,
    width_x,
    inside_ref,
    disp_ref,
    first_ref,
    side_ref,
    corner_ref,
    next_ref,
    high_ref,
    low_ref,
    slot_ref,
    out_ref,
    field_ref,
):
    planes = width_x
    in_x, in_y, in_z = (inside_ref[i] != 0 for i in range(3))
    edges = transposed_lanes(
        jnp.concatenate(
            [
                first_ref[0:1],
                corner_ref[0:1],
                next_ref[15:16],
                next_ref[16:17],
                jnp.zeros((4, LANES), jnp.float32),
            ],
            0,
        )
    )
    sums = {}
    for c in range(3):
        for x in range(planes + 1):
            k = c * planes + x
            if x < planes:
                here = disp_ref[pl.ds(8 * k, 8), :]
                above = next_ref[pl.ds(k, 1), :]
                spot, column = 8 * k, 0
            else:
                here = side_ref[pl.ds(8 * c, 8), :]
                above = next_ref[pl.ds(3 * planes + c, 1), :]
                spot, column = 8 * c * planes, 1
            edge = jnp.where(in_z, edges[spot : spot + 8, column : column + 1], 0.0)
            corner = jnp.where(in_z, edges[spot : spot + 1, column + 2 : column + 3], 0.0)
            if x == planes:
                here, edge = jnp.where(in_x, here, 0.0), jnp.where(in_x, edge, 0.0)
                above, corner = jnp.where(in_x, above, 0.0), jnp.where(in_x, corner, 0.0)
            above, corner = jnp.where(in_y, above, 0.0), jnp.where(in_y, corner, 0.0)
            here_z = jnp.concatenate([here[:, 1:], edge], 1)
            there = jnp.concatenate([here[1:], above], 0)
            there_z = jnp.concatenate([here_z[1:], jnp.concatenate([above[:, 1:], corner], 1)], 0)
            low, high = here + here_z, there + there_z
            sums[c, x] = (low + high, high - low, (here_z - here) + (there_z - there))
    for x in range(planes):
        grad_x = [0.25 * (sums[c, x + 1][0] - sums[c, x][0]) for c in range(3)]
        grad_y = [0.25 * (sums[c, x + 1][1] + sums[c, x][1]) for c in range(3)]
        grad_z = [0.25 * (sums[c, x + 1][2] + sums[c, x][2]) for c in range(3)]
        slot = (slot_ref[pl.ds(8 * x, 8), :] + 1).astype(jnp.float32)
        fields = (
            grad_x[0],
            grad_y[1],
            grad_z[2],
            grad_z[1] + grad_y[2],
            grad_z[0] + grad_x[2],
            grad_y[0] + grad_x[1],
            slot,
        )
        for f, field in enumerate(fields):
            field_ref[pl.ds(8 * (planes * f + x), 8), :] = field
    table = halves(field_ref[...])
    for owner in range(0, owners, STEP):
        steps = range(owner, owner + STEP)
        highs = [spread(high_ref[pl.ds(o, 1), :]) for o in steps]
        columns = low_ref[:, pl.ds(owner * LANES, STEP * LANES)]
        for o, found in zip(steps, looked_up(table, 7, highs, columns)):
            out_ref[pl.ds(7 * o, 7), :] = stacked(found)[0:7]


def tangent_kernel(first, weights_ref, class_ref, blocks_ref, matrix_ref, out_ref, square_ref):
    tangents(first, weights_ref, [], class_ref, blocks_ref, matrix_ref, out_ref, square_ref)


def fetched_tangent_kernel(
    first, weights_hbm, class_ref, blocks_ref, matrix_ref, out_ref, square_ref, weights_ref, sems
):
    chunk = weights_ref.shape[0] // sems.shape[0]
    copies = [
        pltpu.make_async_copy(
            weights_hbm.at[pl.ds(first + chunk * i, chunk)],
            weights_ref.at[pl.ds(chunk * i, chunk)],
            sems.at[i],
        )
        for i in range(sems.shape[0])
    ]
    for copy in copies:
        copy.start()
    tangents(first, weights_ref, copies, class_ref, blocks_ref, matrix_ref, out_ref, square_ref)


def tangents(first, weights_ref, copies, class_ref, blocks_ref, matrix_ref, out_ref, square_ref):
    fibres = blocks_ref[...].astype(jnp.float32)
    gap = jnp.zeros((2, fibres.shape[1]), jnp.float32)
    pieces = []
    for m in range(6):
        pieces += [fibres[6 * m : 6 * m + 6], gap]
    fibres = jnp.concatenate(pieces, 0).astype(jnp.bfloat16)
    square_ref[...] = jnp.zeros(square_ref.shape, jnp.float32)
    square_ref[0:6, 0:6] = matrix_ref[...]
    turned = transposed_lanes(square_ref[...])
    matrix = jnp.concatenate(
        [jnp.broadcast_to(turned[0:8, m : m + 1], (8, LANES)) for m in range(6)], 0
    )
    chunk = 1024
    for i, start in enumerate(range(0, weights_ref.shape[0], chunk)):
        if copies:
            copies[i].wait()
        parts = []
        for group in range(CLASSES):
            columns = slice(LANES * group, LANES * (group + 1))
            parts.append(
                lax.dot_general(
                    fibres[:, columns],
                    weights_ref[pl.ds(start, chunk), columns],
                    NT,
                    preferred_element_type=jnp.float32,
                )
            )
        for block in range(chunk // LANES):
            lanes = slice(LANES * block, LANES * (block + 1))
            level = class_ref[pl.ds((first + start) // LANES + block, 1), :]
            total = parts[0][:, lanes]
            for group in range(1, CLASSES):
                total = total + jnp.where(level >= group, parts[group][:, lanes], 0.0)
            scale = 1.0 / ((level + 1) * LANES).astype(jnp.float32)
            out_ref[:, pl.ds(start + LANES * block, LANES)] = total * scale + matrix


def fields_first(packed_ref, width):
    rows = packed_ref.shape[0] // width
    return halves(
        jnp.concatenate([packed_ref[pl.ds(f, rows, stride=width), :] for f in range(6)], 0)
    )


def respond_kernel(
    arrived_ref, early_ref, late_ref, out_ref, member_ref, lows_ref, answer_ref
):
    owners = arrived_ref.shape[0] // 7
    half = early_ref.shape[1] // LANES
    blocks = 2 * half
    rows = iota((blocks, LANES), 0)
    lane = (iota((blocks, LANES), 1) + 1).astype(jnp.float32)
    slots = []
    for sender in range(owners):
        slot = arrived_ref[pl.ds(7 * sender + 6, 1), :].astype(jnp.int32) - 1
        slots.append(slot)
        named = rows == (slot >> 7)
        columns = pl.ds(sender * LANES, LANES)
        member_ref[pl.ds(0, blocks), columns] = jnp.where(named, float(sender), 0.0).astype(
            jnp.bfloat16
        )
        member_ref[pl.ds(blocks, blocks), columns] = jnp.where(named, lane, 0.0).astype(jnp.bfloat16)
        lows_ref[:, columns] = one_hot(slot & (LANES - 1))
    where = lax.dot_general(
        member_ref[...], lows_ref[...], NT, preferred_element_type=jnp.float32
    ).astype(jnp.int32)

    table = fields_first(arrived_ref, 7)
    for block in range(0, blocks, STEP):
        steps = range(block, block + STEP)
        columns = jnp.concatenate([one_hot(where[blocks + b : blocks + b + 1] - 1) for b in steps], 1)
        found = looked_up(table, 6, [spread(where[b : b + 1]) for b in steps], columns)
        for i, b in enumerate(steps):
            tangent_ref = early_ref if b < half else late_ref
            lanes = pl.ds(b % half * LANES, LANES)
            total = jnp.zeros((8, LANES), jnp.float32)
            for m in range(6):
                total = total + tangent_ref[pl.ds(8 * m, 8), lanes] * found[i][m]
            answer_ref[pl.ds(8 * b, 8), :] = total

    table = fields_first(answer_ref, 8)
    tiles = [answer_ref[pl.ds(8 * b, 8), :] for b in range(blocks)]
    for sender in range(0, owners, STEP + 1):
        steps = range(sender, min(sender + STEP, owners))
        columns = lows_ref[:, pl.ds(sender * LANES, len(steps) * LANES)]
        highs = [spread(slots[s] >> 7) for s in steps]
        for s, found in zip(steps, looked_up(table, 6, highs, columns)):
            out_ref[pl.ds(6 * s, 6), :] = stacked(found)[0:6]
        if sender + STEP < owners:
            s = sender + STEP
            high, low = spread(slots[s] >> 7), spread(slots[s] & (LANES - 1))
            total = jnp.zeros((8, LANES), jnp.float32)
            for b, tile in enumerate(tiles):
                taken = jnp.take_along_axis(tile, low, axis=1, mode="promise_in_bounds")
                total = jnp.where(high == b, taken, total)
            out_ref[pl.ds(6 * s, 6), :] = total[0:6]


def faces_kernel(
    width_x, returned_ref, helper_ref, rank_ref, edge_ref, side_ref, end_ref, last_ref
):
    blocks = helper_ref.shape[0]
    table = fields_first(returned_ref, 6)
    edge = edge_ref[0:2].astype(jnp.int32)
    plane = list(range(blocks - 8, blocks))
    for group in (plane[:4], plane[4:], list(range(7, blocks - 8, 8)) + [blocks]):
        highs, lows = [], []
        for b in group:
            highs.append(spread(helper_ref[pl.ds(b, 1), :] if b < blocks else edge[0:1]))
            lows.append(one_hot(rank_ref[pl.ds(b, 1), :] if b < blocks else edge_ref[1:2]))
        values = looked_up(table, 6, highs, jnp.concatenate(lows, 1))
        for b, found in zip(group, values):
            for f in range(6):
                row = found[f][0:1]
                if b == blocks:
                    continue
                if b >= blocks - 8:
                    side_ref[pl.ds(8 * f + b - blocks + 8, 1), :] = row
                if b % 8 == 7:
                    end_ref[pl.ds(width_x * f + b // 8, 1), :] = row
            if b == blocks:
                part = iota((8, LANES), 1) // blocks
                for half in range(2):
                    row = jnp.zeros((8, LANES), jnp.float32)
                    for g in range(3):
                        row = jnp.where(part == g, found[3 * half + g], row)
                    last_ref[pl.ds(half, 1), :] = row[0:1]
    last_ref[pl.ds(2, 6), :] = jnp.zeros((6, LANES), jnp.float32)


def collect_kernel(returned_ref, helper_ref, rank_ref, sens_ref):
    blocks = helper_ref.shape[0]
    table = fields_first(returned_ref, 6)
    for block in range(0, blocks, STEP):
        steps = range(block, block + STEP)
        highs = [spread(helper_ref[pl.ds(b, 1), :]) for b in steps]
        columns = jnp.concatenate([one_hot(rank_ref[pl.ds(b, 1), :]) for b in steps], 1)
        for i, found in enumerate(looked_up(table, 6, highs, columns)):
            for f in range(6):
                sens_ref[pl.ds(blocks * f + block + i, 1), :] = found[f][0:1]


def force_kernel(width_x, inside_ref, sens_ref, last_ref, side_ref, corner_ref, prior_ref, out_ref):
    planes = width_x
    blocks = 8 * planes
    fields = 6
    in_x, in_y, in_z = (inside_ref[i] != 0 for i in range(3, 6))
    rows = jnp.concatenate(
        [
            last_ref[0:2],
            side_ref[54:56],
            corner_ref[0:2],
            side_ref[56:58],
        ],
        0,
    )
    edges = transposed_lanes(rows)
    sums = {}
    for f in range(fields):
        for x in range(-1, planes):
            part, g = f // 3, f % 3
            if x >= 0:
                here = sens_ref[pl.ds(blocks * f + 8 * x, 8), :]
                above = prior_ref[pl.ds(planes * f + x, 1), :]
                spot, column = blocks * g + 8 * x, part
            else:
                here = side_ref[pl.ds(8 * f, 8), :]
                above = side_ref[pl.ds(8 * fields + f, 1), :]
                spot, column = blocks * g + 8 * (planes - 1), part + 2
            edge = jnp.where(in_z, edges[spot : spot + 8, column : column + 1], 0.0)
            corner = jnp.where(in_z, edges[spot + 7 : spot + 8, column + 4 : column + 5], 0.0)
            if x < 0:
                here, edge = jnp.where(in_x, here, 0.0), jnp.where(in_x, edge, 0.0)
                above, corner = jnp.where(in_x, above, 0.0), jnp.where(in_x, corner, 0.0)
            above, corner = jnp.where(in_y, above, 0.0), jnp.where(in_y, corner, 0.0)
            here_z = jnp.concatenate([edge, here[:, :-1]], 1)
            there = jnp.concatenate([above, here[:-1]], 0)
            there_z = jnp.concatenate([jnp.concatenate([corner, above[:, :-1]], 1), here_z[:-1]], 0)
            low, high = there + there_z, here + here_z
            sums[f, x] = (low + high, low - high, (here_z - here) + (there_z - there))

    def both(f, x, kind):
        return sums[f, x][kind] + sums[f, x - 1][kind]

    def jump(f, x):
        return sums[f, x - 1][0] - sums[f, x][0]

    along = ((0, 5, 4), (5, 1, 3), (4, 3, 2))
    for d in range(3):
        for x in range(planes):
            force = jump(along[d][0], x) + both(along[d][1], x, 1) + both(along[d][2], x, 2)
            out_ref[pl.ds(blocks * d + 8 * x, 8), :] = 0.25 * force


def per_device(
    adjoint_disp, matrix_tangent, fibre_blocks, fibre_weights, rve_class, rve_helper, rve_slot
):
    owners = lax.axis_size("gx") * lax.axis_size("gy")
    width_x, width_y, width_z = adjoint_disp.shape[1:]
    points = width_x * width_y * width_z
    blocks = points // LANES
    fibres = fibre_weights.shape[1]
    places = [lax.axis_index(axis) for axis in ("gx", "gy", "gz")]
    ends = [lax.axis_size(axis) - 1 for axis in ("gx", "gy", "gz")]
    inside = jnp.stack(
        [place < end for place, end in zip(places, ends)] + [place > 0 for place in places]
    ).astype(jnp.int32)

    with jax.named_scope("fetch"):
        inputs = (
            adjoint_disp.reshape(3 * blocks, LANES),
            rve_helper.reshape(blocks, LANES),
            rve_slot.reshape(blocks, LANES),
            rve_class.reshape(blocks, LANES),
            matrix_tangent,
        )
        kept = [jax.ShapeDtypeStruct(a.shape, a.dtype) for a in inputs]
        first, disp, helper, slot, level, matrix = whole_call(
            functools.partial(fetch_kernel, len(inputs)),
            "fetch",
            [f32(8, LANES)] + kept,
            [pltpu.with_memory_space_constraint(a, pltpu.HBM) for a in inputs],
            [pltpu.SemaphoreType.DMA((len(inputs),))],
            places=[HBM] * len(inputs),
        )
        disp_grid = disp.reshape(3, width_x, width_y, LANES)

    with jax.named_scope("route"):
        weights_hbm = pltpu.with_memory_space_constraint(fibre_weights, pltpu.HBM)
        high, low, rank, edge, weights = whole_call(
            functools.partial(route_kernel, owners),
            "route",
            [
                i32(owners, LANES),
                jax.ShapeDtypeStruct((LANES, owners * LANES), jnp.bfloat16),
                f32(blocks, LANES),
                f32(8, LANES),
                jax.ShapeDtypeStruct((points // 2, fibres), fibre_weights.dtype),
            ],
            (helper, weights_hbm),
            [
                pltpu.VMEM((2 * owners, points), jnp.bfloat16),
                pltpu.VMEM((LANES, points), jnp.bfloat16),
                pltpu.SemaphoreType.DMA(()),
            ],
            flops=2 * points * LANES * 2 * owners,
            places=[VMEM, HBM],
        )

    with jax.named_scope("tangent"):
        half = points // 2
        early = whole_call(
            functools.partial(tangent_kernel, 0),
            "early_tangent",
            f32(48, half),
            (weights, level, fibre_blocks, matrix),
            [pltpu.VMEM((8, LANES), jnp.float32)],
            flops=256 * points * fibres,
        )
        late = whole_call(
            functools.partial(fetched_tangent_kernel, half),
            "late_tangent",
            f32(48, half),
            (weights_hbm, level, fibre_blocks, matrix),
            [
                pltpu.VMEM((8, LANES), jnp.float32),
                pltpu.VMEM((half, fibres), jnp.bfloat16),
                pltpu.SemaphoreType.DMA((2,)),
            ],
            flops=256 * points * fibres,
            places=[HBM, VMEM, VMEM, VMEM],
        )

    with jax.named_scope("lift"):
        side = passed_round(disp_grid[:, 0].reshape(24, LANES), ("gx",), -1)
        corner = passed_round(first, ("gx", "gz"), -1)
        first = passed_round(first, ("gz",), -1)
        side, corner, first, high, low, rank, edge, early, inside = lax.optimization_barrier(
            (side, corner, first, high, low, rank, edge, early, inside)
        )
        next_y = jnp.concatenate(
            [
                disp_grid[:, :, 0].reshape(3 * width_x, LANES),
                side[0:24:8],
                first[0:1],
                corner[0:1],
            ],
            0,
        )
        next_y = passed_round(next_y, ("gy",), -1)
        next_y, late = lax.optimization_barrier((next_y, late))

    with jax.named_scope("strain"):
        buckets = whole_call(
            functools.partial(strain_kernel, owners, width_x),
            "strain",
            f32(owners * 7, LANES),
            (inside, disp, first, side, corner, next_y, high, low, slot),
            [pltpu.VMEM((7 * blocks, LANES), jnp.float32)],
            places=[SMEM] + [VMEM] * 8,
        )

    with jax.named_scope("exchange"):
        arrived = exchanged(buckets, owners, ("gx", "gy"))

    with jax.named_scope("respond"):
        answer = whole_call(
            respond_kernel,
            "respond",
            f32(owners * 6, LANES),
            (arrived, early, late),
            [
                pltpu.VMEM((2 * blocks, owners * LANES), jnp.bfloat16),
                pltpu.VMEM((LANES, owners * LANES), jnp.bfloat16),
                pltpu.VMEM((8 * blocks, LANES), jnp.float32),
            ],
        )

    with jax.named_scope("return"):
        returned = exchanged(answer, owners, ("gx", "gy"))

    with jax.named_scope("collect"):
        side, end, last = whole_call(
            functools.partial(faces_kernel, width_x),
            "faces",
            [f32(48, LANES), f32(6 * width_x, LANES), f32(8, LANES)],
            (returned, helper, rank, edge),
        )
        sens = whole_call(
            collect_kernel,
            "collect",
            f32(6 * blocks, LANES),
            (returned, helper, rank),
        )

    with jax.named_scope("settle"):
        prior = passed_round(end, ("gy",), 1)
        corner = passed_on(last, ("gy", "gz"), 1)
        last = passed_round(last, ("gz",), 1)
        side = jnp.concatenate(
            [side, prior[width_x - 1 : 6 * width_x : width_x], last[0:2], corner[0:2]], 0
        )
        side = passed_on(side, ("gx",), 1)
        side, sens = lax.optimization_barrier((side, sens))
        force = whole_call(
            functools.partial(force_kernel, width_x),
            "force",
            f32(3 * blocks, LANES),
            (inside, sens, last, side, corner, prior),
            places=[SMEM] + [VMEM] * 5,
        )
    return force.reshape(3, width_x, width_y, width_z)


def solution(mesh):
    in_specs = (
        P(None, "gx", "gy", "gz"),
        P(),
        P(),
        P(("gx", "gy", "gz"), None),
        P(("gx", "gy", "gz")),
        P("gx", "gy", "gz"),
        P("gx", "gy", "gz"),
    )
    out_specs = P(None, "gx", "gy", "gz")
    return jax.shard_map(
        per_device, mesh=mesh, in_specs=in_specs, out_specs=out_specs, check_vma=False
    )
```
